128 devices in a mesh: row: 16 (over x, y), col: 8 (over z, core).
Axes of the slice: x: 4, y: 4, z: 4, core: 2. Of those that a mesh axis runs over, the one named last changes fastest.
Arguments:
- amp_store: bfloat16 [32768, 1024], P(('row', 'col')), may hold values from -6 to 6
- store_map: int32 [32768], P(('row', 'col')), may hold values from 0 to 32767, as said below
- integrals: bfloat16 [32768, 32768], P('row', 'col'), may hold values from -0.09375 to 0.09375
- occ_irrep: int32 [100], replicated, may hold values from 0 to 7
- virt_irrep: int32 [800], replicated, may hold values from 0 to 7
- occ_orbs: int32 [2, 1024], replicated, may hold values from 0 to 99
- k_orbs: int32 [2, 32768], P(None, 'col'), may hold values from 0 to 799
- m_orbs: int32 [2, 32768], P(None, 'row'), may hold values from 0 to 799
Outputs:
- ladder: bfloat16 [32768, 1024], P('row', 'col')
The draws below stay inside these ranges and needn't reach their ends.
Inputs may be any that keep to these rules, and one draw needn't show every extreme that they name: store_map is a permutation. Grid position k belongs to the block of device (r, c) with c = k // 4096 and r = (k % 4096) // 256; the stored rows of device s = r' * 8 + c' (its shard of amp_store) send exactly 2 rows to every device's block, and within block (r, c) those rows fill positions s * 2 to s * 2 + 1.
All inputs are finite; a program needn't handle non-finite values.
Results may differ from the reference program's by a relative error of at most 0.001.
Values may be sent and summed in bfloat16 or wider, within the bound.
No kernel may reach another device: no remote copies, remote signals or barrier semaphores. Data moves between devices by JAX's collectives and lax.ppermute only.
A program may use at most 192 MiB of HBM per device.

```python
import jax
import jax.numpy as jnp
from jax import lax

NOCC = 100
NVIRT = 800
PAIRS = 1024
M_DEV = 2048
SLOT = 2
GRID_ROWS = 16
GRID_COLS = 8
STORE_ROWS = 256
KPAIRS = 32768
KBLOCK = 4096
MPAIRS = 32768
N_ROW = 16


def draw_store_map(key, part):
    dev_count = GRID_ROWS * GRID_COLS
    keys = jax.random.split(key, dev_count)
    orders = jax.vmap(lambda single: jax.random.permutation(single, STORE_ROWS))(keys)
    target = orders // SLOT
    within = orders % SLOT
    source = jnp.arange(dev_count, dtype=jnp.int32)[:, None]
    target_row = target // GRID_COLS
    target_col = target % GRID_COLS
    position = target_col * KBLOCK + target_row * STORE_ROWS + source * SLOT + within
    return position.reshape(-1).astype(jnp.int32)


def place_ends(array, key, low, largest):
    place = [jax.random.randint(jax.random.fold_in(key, axis), (), 0, length) for axis, length in enumerate(array.shape)]
    widest = array.shape.index(max(array.shape))
    beside = place[:widest] + [(place[widest] + 1) % array.shape[widest]] + place[widest + 1:]
    return array.at[tuple(place)].set(low).at[tuple(beside)].set(largest)


def block_scale(key, extent, cuts, low, high):
    loudness, own = 1.0, jax.random.fold_in(key, 6)
    for dim, shards_of in cuts:
        draws = jnp.exp(jax.random.uniform(jax.random.fold_in(own, dim), (shards_of,), jnp.float32, low / len(cuts), high / len(cuts)))
        loudness = loudness * jnp.repeat(draws, extent[dim] // shards_of).reshape([-1 if axis == dim else 1 for axis in range(len(extent))])
    return loudness


def normal_values(stream_key, extent, scale, limit, cuts=(), kind=jnp.bfloat16):
    values = scale * jax.random.normal(stream_key, extent, jnp.float32)
    if cuts:
        values = values * block_scale(stream_key, extent, cuts, -0.22, 0.18)
    return jnp.clip(values, -limit, limit).astype(kind)


def setup_inputs(seed: int = 0) -> dict:
    arg_keys = jax.random.split(jax.random.key(seed), 9)
    return {
        "amp_store": normal_values(arg_keys[0], (KPAIRS, PAIRS), 1.0, 6.0, ((0, 128),)),
        "store_map": draw_store_map(jax.random.fold_in(arg_keys[8], 71), 0),
        "integrals": normal_values(arg_keys[2], (MPAIRS, KPAIRS), (KPAIRS // 8) ** -0.5, 0.09375, ((0, 16), (1, 8))),
        "occ_irrep": place_ends(jax.random.randint(arg_keys[3], (NOCC,), 0, 8), jax.random.fold_in(arg_keys[3], 1), 0, 7).astype(jnp.int32),
        "virt_irrep": place_ends(jax.random.randint(arg_keys[4], (NVIRT,), 0, 8), jax.random.fold_in(arg_keys[4], 1), 0, 7).astype(jnp.int32),
        "occ_orbs": place_ends(jax.random.randint(arg_keys[5], (2, PAIRS), 0, NOCC), jax.random.fold_in(arg_keys[5], 1), 0, NOCC - 1).astype(jnp.int32),
        "k_orbs": place_ends(jax.random.randint(arg_keys[6], (2, KPAIRS), 0, NVIRT), jax.random.fold_in(arg_keys[6], 1), 0, NVIRT - 1).astype(jnp.int32),
        "m_orbs": place_ends(jax.random.randint(arg_keys[7], (2, MPAIRS), 0, NVIRT), jax.random.fold_in(arg_keys[7], 1), 0, NVIRT - 1).astype(jnp.int32),
    }


def pair_irrep(labels, orbitals):
    return jnp.bitwise_xor(labels[orbitals[0]], labels[orbitals[1]])


def reference(amp_store, store_map, integrals, occ_irrep, virt_irrep, occ_orbs, k_orbs, m_orbs):
    amplitudes = jnp.zeros(amp_store.shape, amp_store.dtype).at[store_map].set(amp_store)
    occ_sym = pair_irrep(occ_irrep, occ_orbs)
    k_sym = pair_irrep(virt_irrep, k_orbs)
    m_sym = pair_irrep(virt_irrep, m_orbs)
    naught = jnp.zeros((), amp_store.dtype)
    kept = jnp.where(k_sym[:, None] == occ_sym[None, :], amplitudes, naught)
    blocks = integrals.reshape(N_ROW, M_DEV, KPAIRS)
    block_sym = m_sym.reshape(N_ROW, M_DEV)

    def one_block(inputs):
        values, symbols = inputs
        screened = jnp.where(symbols[:, None] == k_sym[None, :], values, naught)
        return jnp.dot(screened, kept, preferred_element_type=jnp.float32).astype(jnp.bfloat16)

    result = lax.map(one_block, (blocks, block_sym))
    return result.reshape(MPAIRS, PAIRS)
```

```python
import functools

import jax
import jax.numpy as jnp
from jax import lax
from jax.experimental import pallas as pl
from jax.experimental.pallas import tpu as pltpu
from jax.sharding import PartitionSpec as P

BF16 = jnp.bfloat16
F32 = jnp.float32
I32 = jnp.int32
LANES = 128
CAP = 32
TM = 256
VMEM_LIMIT = 48 * 1024 * 1024


def pack_labels(labels):
    word = labels[0:1, :]
    for i in range(1, labels.shape[0]):
        word = word | (labels[i : i + 1, :] << (4 * i))
    return jnp.broadcast_to(word, (8, LANES))


def look_up(packed, orbitals):
    orbitals = jnp.broadcast_to(orbitals, (8, LANES))
    word = jnp.take_along_axis(packed, orbitals & (LANES - 1), axis=1)
    return (word >> ((orbitals >> 7) << 2)) & 7


def pair_symbols(packed, orbs_ref, start):
    lanes = slice(start, start + LANES)
    return look_up(packed, orbs_ref[0:1, lanes]) ^ look_up(packed, orbs_ref[1:2, lanes])


def as_column(symbols):
    row = jnp.broadcast_to(symbols[0:1, :].astype(F32), (LANES, LANES))
    return jnp.transpose(row)


def symbols_kernel(
    occ_ref, virt_ref, occ_orbs, k_orbs, m_orbs, own_orbs, occ_out, rank_out, k_out, m_out, own_out, most_out
):
    occ = pack_labels(occ_ref[0:1, :])
    virt = pack_labels(virt_ref[0:7, :])
    first = lax.broadcasted_iota(I32, (LANES, LANES), 0)
    second = lax.broadcasted_iota(I32, (LANES, LANES), 1)
    most = jnp.zeros((1, LANES), I32)
    for start in range(0, occ_orbs.shape[1], LANES):
        sym = pair_symbols(occ, occ_orbs, start)
        occ_out[:, start : start + LANES] = sym
        same = as_column(sym) == jnp.broadcast_to(sym[0:1, :].astype(F32), (LANES, LANES))
        earlier = jnp.where(same & (first < second), 1.0, 0.0)
        rank = jnp.sum(earlier, axis=0, keepdims=True).astype(I32)
        most = jnp.maximum(most, rank)
        rank_out[:, start : start + LANES] = jnp.broadcast_to(rank, (8, LANES))
    most_out[0, 0] = jnp.max(most)
    for start in range(0, k_orbs.shape[1], LANES):
        sym = pair_symbols(virt, k_orbs, start).astype(F32)
        k_out[:, start : start + LANES] = jnp.concatenate([sym, sym], axis=0).astype(BF16)
    for start in range(0, m_orbs.shape[1], LANES):
        m_out[start : start + LANES, :] = as_column(pair_symbols(virt, m_orbs, start)).astype(BF16)
    for start in range(0, own_orbs.shape[1], LANES):
        own_out[start : start + LANES, :] = as_column(pair_symbols(virt, own_orbs, start)).astype(I32)


def compact_kernel(copies, pass_ref, rows_ref, own_ref, occ_ref, rank_ref, out_ref):
    n, pairs = rows_ref.shape
    cols = pairs // LANES
    i = lax.broadcasted_iota(I32, (n, n), 0)
    j = lax.broadcasted_iota(I32, (n, n), 1)
    wanted = ((i >> 1) & 7) * 32 + (i >> 4) * 2 + (i & 1)
    order = jnp.where(j == wanted, 1.0, 0.0).astype(BF16)
    rows = jnp.dot(order, rows_ref[...], preferred_element_type=F32)
    base = pass_ref[0] * CAP
    slot = lax.broadcasted_iota(I32, (CAP, LANES), 0) + base
    own = own_ref[...]
    for c in range(cols):
        lanes = slice(c * LANES, (c + 1) * LANES)
        keep = own == jnp.broadcast_to(occ_ref[0:1, lanes], (n, LANES))
        kept = jnp.where(keep, rows[:, lanes], 0.0).astype(BF16)
        pick = jnp.where(slot == jnp.broadcast_to(rank_ref[0:1, lanes], (CAP, LANES)), 1.0, 0.0).astype(BF16)
        part = lax.dot_general(kept, pick, (((1,), (1,)), ((), ())), preferred_element_type=F32).astype(BF16)
        for r in range(copies):
            out_ref[r, :, c * CAP : (c + 1) * CAP] = part


def product_kernel(core_ref, amp_ref, int_ref, k_ref, m_ref, keep_ref, send_ref, kept):
    depth, width = amp_ref.shape
    block = depth // 16

    @pl.when(pl.program_id(0) == 0)
    def _():
        for r in range(16):
            for source in range(16):
                kept[r * block + source * 16 : r * block + source * 16 + 16, :] = amp_ref[
                    source * block + r * 16 : source * block + r * 16 + 16, :
                ]

    m_sym = m_ref[...]
    chunk = 1024
    total = jnp.zeros((m_ref.shape[0], width), F32)
    for at in range(0, depth, chunk):
        parts = []
        for lane in range(at, at + chunk, LANES):
            lanes = slice(lane, lane + LANES)
            same = m_sym == jnp.broadcast_to(k_ref[0:1, lanes], m_sym.shape)
            parts.append(jnp.where(same, int_ref[:, lanes], jnp.zeros((), BF16)))
        screened = jnp.concatenate(parts, axis=1)
        total += jnp.dot(screened, kept[at : at + chunk, :], preferred_element_type=F32)
    turned = jnp.transpose(total)
    even = core_ref[0] == 0
    for z in range(4):
        low = turned[z * 2 * CAP : z * 2 * CAP + CAP, :]
        high = turned[z * 2 * CAP + CAP : z * 2 * CAP + 2 * CAP, :]
        keep_ref[z] = jnp.where(even, low, high)
        send_ref[z] = jnp.where(even, high, low)


def share_kernel(z_ref, keep_ref, got_ref, *out_refs):
    for step, out_ref in enumerate(out_refs):
        z = (z_ref[0] + step) % 4
        out_ref[...] = keep_ref[z] + got_ref[z]


def expand_kernel(at_ref, a_ref, b_ref, c_ref, d_ref, m_ref, occ_ref, rank_ref, out_ref):
    lanes = pl.ds(pl.multiple_of(at_ref[0] * LANES, LANES), LANES)
    total = (a_ref[...] + b_ref[...] + c_ref[...] + d_ref[...]).astype(BF16)
    slot = lax.broadcasted_iota(I32, (CAP, LANES), 0) + at_ref[1] * CAP
    pick = jnp.where(slot == jnp.broadcast_to(rank_ref[0:1, lanes], (CAP, LANES)), 1.0, 0.0).astype(BF16)
    wide = lax.dot_general(total, pick, (((0,), (0,)), ((), ())), preferred_element_type=F32)
    same = m_ref[...].astype(F32) == jnp.broadcast_to(occ_ref[0:1, lanes].astype(F32), wide.shape)
    out_ref[...] = jnp.where(same, wide, 0.0).astype(BF16)


def params():
    return pltpu.CompilerParams(vmem_limit_bytes=VMEM_LIMIT)


def whole():
    return pl.BlockSpec(memory_space=pltpu.VMEM)


def scalars():
    return pl.BlockSpec(memory_space=pltpu.SMEM)


def body(amp_store, store_map, integrals, occ_irrep, virt_irrep, occ_orbs, k_orbs, m_orbs):
    rows = lax.axis_size("row")
    cols = lax.axis_size("col")
    stored, pairs = amp_store.shape
    kblock = k_orbs.shape[1]
    m_dev = m_orbs.shape[1]
    my_row = lax.axis_index("row")
    my_col = lax.axis_index("col")
    shape = jax.ShapeDtypeStruct

    place = (store_map // kblock) * (rows * 2) + ((store_map % kblock) // stored) * 2 + store_map % 2
    order = (jnp.arange(stored, dtype=I32)[:, None] == place[None, :]).astype(BF16)
    ordered = jnp.dot(order, amp_store, preferred_element_type=F32).astype(BF16)
    column_rows = lax.all_to_all(ordered, "col", split_axis=0, concat_axis=0, tiled=True)

    own_orbs = lax.dynamic_slice_in_dim(k_orbs.reshape(2, rows, stored), my_row * 16, 16, axis=2).reshape(2, stored)
    occ_lab = jnp.pad(occ_irrep, (0, LANES - occ_irrep.shape[0])).reshape(1, LANES)
    virt_lab = jnp.pad(virt_irrep, (0, 8 * LANES - virt_irrep.shape[0])).reshape(8, LANES)
    occ_sym, rank, k_sym, m_sym, own_sym, most = pl.pallas_call(
        symbols_kernel,
        out_shape=(
            shape((8, pairs), I32),
            shape((8, pairs), I32),
            shape((16, kblock), BF16),
            shape((m_dev, LANES), BF16),
            shape((stored, LANES), I32),
            shape((1, 1), I32),
        ),
        in_specs=[whole()] * 6,
        out_specs=(whole(),) * 5 + (scalars(),),
        compiler_params=params(),
        name="symbols",
    )(occ_lab, virt_lab, occ_orbs, k_orbs, m_orbs, own_orbs)

    def one_pass(step):
        width = cols * CAP
        compact = pl.pallas_call(
            functools.partial(compact_kernel, rows),
            out_shape=shape((rows, stored, width), BF16),
            in_specs=[scalars()] + [whole()] * 4,
            out_specs=whole(),
            compiler_params=params(),
            name="compact",
        )(step.reshape(1), column_rows, own_sym, occ_sym, rank)
        gathered = lax.all_to_all(
            compact.reshape(rows * stored, width), "row", split_axis=0, concat_axis=0, tiled=True
        )
        keep, send = pl.pallas_call(
            product_kernel,
            grid=(m_dev // TM,),
            out_shape=(shape((4, CAP, m_dev), F32),) * 2,
            in_specs=[
                scalars(),
                pl.BlockSpec((kblock, width), lambda i: (0, 0)),
                pl.BlockSpec((TM, kblock), lambda i: (i, 0)),
                pl.BlockSpec((16, kblock), lambda i: (0, 0)),
                pl.BlockSpec((TM, LANES), lambda i: (i, 0)),
            ],
            out_specs=(pl.BlockSpec((4, CAP, TM), lambda i: (0, 0, i)),) * 2,
            scratch_shapes=[pltpu.VMEM((kblock, width), BF16)],
            compiler_params=params(),
            name="product",
        )((my_col % 2).reshape(1), gathered, integrals, k_sym, m_sym)
        got = lax.ppermute(send, "col", [(i, i ^ 1) for i in range(cols)])
        shares = pl.pallas_call(
            share_kernel,
            out_shape=(shape((CAP, m_dev), F32),) * 4,
            in_specs=[scalars(), whole(), whole()],
            out_specs=(whole(),) * 4,
            compiler_params=params(),
            name="share",
        )((my_col // 2).reshape(1), keep, got)
        sums = [shares[0]]
        for distance in range(1, 4):
            hops = [(i, (i + 2 * distance) % cols) for i in range(cols)]
            sums.append(lax.ppermute(shares[distance], "col", hops))
        return pl.pallas_call(
            expand_kernel,
            out_shape=shape((m_dev, LANES), BF16),
            in_specs=[scalars()] + [whole()] * 7,
            out_specs=whole(),
            compiler_params=params(),
            name="expand",
        )(jnp.stack([my_col, step]), *sums, m_sym, occ_sym, rank)

    passes = most[0, 0] // CAP + 1
    first = one_pass(jnp.zeros((), I32))
    return lax.while_loop(
        lambda state: state[0] < passes,
        lambda state: (state[0] + 1, state[1] + one_pass(state[0])),
        (jnp.ones((), I32), first),
    )[1]


def solution(mesh):
    in_specs = (
        P(("row", "col"), None),
        P(("row", "col")),
        P("row", "col"),
        P(),
        P(),
        P(),
        P(None, "col"),
        P(None, "row"),
    )
    out_specs = P("row", "col")
    return jax.shard_map(body, mesh=mesh, in_specs=in_specs, out_specs=out_specs, check_vma=False)
```

```python
import functools

import jax
import jax.numpy as jnp
from jax import lax
from jax.experimental import pallas as pl
from jax.experimental.pallas import tpu as pltpu
from jax.sharding import PartitionSpec as P

BF16 = jnp.bfloat16
F32 = jnp.float32
I32 = jnp.int32
LANES = 128
CAP = 32
BASE = 16
SPILL = 48
PLACES = 8 * BASE + SPILL
TM = 256


def pack_labels(labels):
    word = labels[0:1, :]
    for i in range(1, labels.shape[0]):
        word = word | (labels[i : i + 1, :] << (4 * i))
    return jnp.broadcast_to(word, (8, LANES))


def look_up(packed, orbitals):
    orbitals = jnp.broadcast_to(orbitals, (8, LANES))
    word = jnp.take_along_axis(packed, orbitals & (LANES - 1), axis=1)
    return (word >> ((orbitals >> 7) << 2)) & 7


def pair_symbols(packed, orbs_ref, start):
    lanes = slice(start, start + LANES)
    return look_up(packed, orbs_ref[0:1, lanes]) ^ look_up(packed, orbs_ref[1:2, lanes])


def as_column(symbols):
    row = jnp.broadcast_to(symbols[0:1, :].astype(F32), (LANES, LANES))
    return jnp.transpose(row)


def one_hot(mask):
    return jnp.where(mask, 1.0, 0.0).astype(BF16)


def rows_dot(a, b):
    return lax.dot_general(a, b, (((1,), (1,)), ((), ())), preferred_element_type=F32)


def iota(shape, axis):
    return lax.broadcasted_iota(I32, shape, axis)


def order_kernel(map_ref, amp_ref, *out_refs):
    z, core = lax.axis_index("col") >> 1, lax.axis_index("col") & 1
    k = map_ref[...]
    col, row, within = k >> 12, (k >> 8) & 15, k & 1
    place = ((((col >> 1) - z) & 3) * 2 + ((col & 1) ^ core)) * 32 + row * 2 + within
    n = amp_ref.shape[0]
    order = one_hot(iota((n, n), 0) == jnp.broadcast_to(place, (n, n)))
    rows = jnp.dot(order, amp_ref[...], preferred_element_type=F32).astype(BF16)
    for d, out_ref in enumerate(out_refs):
        out_ref[...] = rows[d * 64 : d * 64 + 64, :]


def symbols_kernel(
    occ_ref, virt_ref, occ_orbs, k_orbs, m_orbs, own_orbs, other_orbs,
    occ_out, rank_out, place_out, spread_out, k_out, k_col_out, m_out, own_out, other_out, bad_out,
):
    core = lax.axis_index("col") & 1
    occ = pack_labels(occ_ref[0:1, :])
    virt = pack_labels(virt_ref[0:7, :])
    first = iota((LANES, LANES), 0)
    second = iota((LANES, LANES), 1)
    group = iota((8, LANES), 0)
    used = jnp.zeros((8, 1), I32)
    bad = jnp.zeros((1, LANES), I32)
    for c in range(occ_orbs.shape[1] // LANES):
        lanes = slice(c * LANES, (c + 1) * LANES)
        sym = pair_symbols(occ, occ_orbs, c * LANES)
        occ_out[:, lanes] = sym
        same = as_column(sym) == jnp.broadcast_to(sym[0:1, :].astype(F32), (LANES, LANES))
        rank = jnp.sum(jnp.where(same & (first < second), 1.0, 0.0), axis=0, keepdims=True).astype(I32)
        rank_out[:, lanes] = jnp.broadcast_to(rank, (8, LANES))
        mine = sym == group
        extra = jnp.sum(jnp.where(mine, used, 0), axis=0, keepdims=True) + rank - BASE
        used = used + jnp.maximum(jnp.sum(jnp.where(mine, 1, 0), axis=1, keepdims=True) - BASE, 0)
        spilt = rank >= BASE
        bad = jnp.maximum(bad, jnp.where(spilt & ((extra >= SPILL) | (rank >= CAP - 1)), 1, 0))
        fits = spilt & (extra < SPILL)
        place = jnp.where(spilt, jnp.where(fits, 8 * BASE + extra, -1), c * BASE + rank)
        place_out[:, lanes] = jnp.broadcast_to(place, (8, LANES))
        at = jnp.where(spilt, rank - BASE, -1)
        entry = jnp.where(fits, sym[0:1, :] * SPILL + extra, -1)
        to = one_hot(iota((BASE, LANES), 0) == jnp.broadcast_to(at, (BASE, LANES)))
        source = one_hot(iota((8 * SPILL, LANES), 0) == jnp.broadcast_to(entry, (8 * SPILL, LANES)))
        spread_out[c * BASE : (c + 1) * BASE, :] = rows_dot(to, source).astype(BF16)
    bad_out[0, 0] = jnp.max(bad)
    for start in range(0, k_orbs.shape[1], LANES):
        sym = pair_symbols(virt, k_orbs, start)
        wide = sym.astype(F32)
        k_out[:, start : start + LANES] = jnp.concatenate([wide, wide], axis=0).astype(BF16)
        k_col_out[start : start + LANES, :] = as_column(sym).astype(BF16)
    for start in range(0, m_orbs.shape[1], LANES):
        m_out[start : start + LANES, :] = as_column(pair_symbols(virt, m_orbs, start)).astype(BF16)
    i, j = iota((LANES, 2 * LANES), 0), iota((LANES, 2 * LANES), 1)
    pick = one_hot(j == (i >> 1) * 4 + core * 2 + (i & 1))
    for orbs, out in ((own_orbs, own_out), (other_orbs, other_out)):
        column = jnp.concatenate([as_column(pair_symbols(virt, orbs, s)) for s in (0, LANES)], axis=0)
        out[...] = jnp.dot(pick, column.astype(BF16), preferred_element_type=F32)


def compact_kernel(a_ref, b_ref, c_ref, d_ref, own_ref, other_ref, occ_ref, place_ref, mine_out, theirs_out):
    z = lax.axis_index("col") >> 1
    rows = jnp.concatenate([a_ref[...], b_ref[...], c_ref[...], d_ref[...]], axis=0)
    pairs = rows.shape[1]
    squeeze = one_hot(iota((PLACES, pairs), 0) == jnp.broadcast_to(place_ref[0:1, :], (PLACES, pairs)))
    occ = jnp.broadcast_to(occ_ref[0:1, :].astype(F32), (LANES, pairs))
    i, j = iota((LANES, 2 * LANES), 0), iota((LANES, 2 * LANES), 1)
    row, source, within = i >> 3, (i >> 1) & 3, i & 1
    for side, sym_ref, out in ((0, own_ref, mine_out), (1, other_ref, theirs_out)):
        order = one_hot(j == (((z - source) & 3) * 2 + side) * 32 + row * 2 + within)
        turned = jnp.dot(order, rows, preferred_element_type=F32)
        sym = jnp.concatenate([sym_ref[...]] * (pairs // LANES), axis=1)
        kept = jnp.where(sym == occ, turned, 0.0).astype(BF16)
        out[...] = rows_dot(squeeze, kept).astype(BF16)


def product_kernel(amp_ref, int_ref, k_ref, k_col_ref, m_ref, spread_ref, keep_ref, send_ref, kept):
    core = lax.axis_index("col") & 1
    depth = k_ref.shape[1]

    @pl.when(pl.program_id(0) == 0)
    def _():
        i, j = iota((256, 256), 0), iota((256, 256), 1)
        lane = (((i >> 1) & 1) ^ core) * 128 + (i >> 4) * 8 + ((i >> 2) & 3) * 2 + (i & 1)
        order = one_hot(j == lane)
        spread = spread_ref[...]
        entry = iota((256, LANES), 1)
        for source in range(16):
            slots = amp_ref[source]
            stack = jnp.concatenate([slots[: 8 * BASE]] + [slots[8 * BASE :]] * 8, axis=0)
            block = rows_dot(order, stack)
            sym = jnp.concatenate(
                [k_col_ref[r * 256 + source * 16 : r * 256 + source * 16 + 16, :] for r in range(16)], axis=0
            ).astype(F32)
            parts = []
            for t in range(8 * SPILL // LANES):
                low = sym * SPILL - t * LANES
                at = entry.astype(F32)
                inside = (at >= low) & (at < low + SPILL)
                part = block[:, 8 * BASE + t * LANES : 8 * BASE + (t + 1) * LANES]
                parts.append(jnp.where(inside, part, 0.0).astype(BF16))
            spilt = rows_dot(jnp.concatenate(parts, axis=1), spread).astype(BF16)
            both = jnp.concatenate([block[:, : 8 * BASE].astype(BF16), spilt], axis=1)
            for r in range(16):
                kept[r * 256 + source * 16 : r * 256 + source * 16 + 16, :] = both[r * 16 : r * 16 + 16, :]

    m_sym = m_ref[...]
    chunk = 1024
    total = jnp.zeros((m_ref.shape[0], 256), F32)
    for at in range(0, depth, chunk):
        parts = []
        for lane in range(at, at + chunk, LANES):
            lanes = slice(lane, lane + LANES)
            same = m_sym == jnp.broadcast_to(k_ref[0:1, lanes], m_sym.shape)
            parts.append(jnp.where(same, int_ref[:, lanes], jnp.zeros((), BF16)))
        screened = jnp.concatenate(parts, axis=1)
        total += jnp.dot(screened, kept[at : at + chunk, :], preferred_element_type=F32)
    turned = jnp.transpose(total)
    even = core == 0
    for z in range(4):
        for half in range(2):
            at = half * 128 + z * 2 * BASE
            low, high = turned[at : at + BASE, :], turned[at + BASE : at + 2 * BASE, :]
            rows = slice(half * BASE, half * BASE + BASE)
            keep_ref[z, rows, :] = jnp.where(even, low, high)
            send_ref[z, rows, :] = jnp.where(even, high, low)


def share_kernel(keep_ref, got_ref, own_ref, *out_refs):
    z = lax.axis_index("col") >> 1
    own_ref[...] = keep_ref[z] + got_ref[z]
    for step, out_ref in enumerate(out_refs):
        there = (z + step + 1) & 3
        total = keep_ref[there] + got_ref[there]
        largest = jnp.max(jnp.abs(total), axis=0, keepdims=True)
        power = jnp.minimum(jnp.floor(14.9 - jnp.log2(jnp.maximum(largest, 1e-37))), 120.0)
        scaled = total * jnp.exp2(power)
        scaled = jnp.where(iota(total.shape, 0) == CAP - 1, power, scaled)
        out_ref[...] = (scaled + jnp.where(scaled >= 0, 0.5, -0.5)).astype(I32).astype(jnp.int16)


def expand_kernel(own_ref, a_ref, b_ref, c_ref, m_ref, occ_ref, rank_ref, out_ref):
    lanes = pl.ds(pl.multiple_of(lax.axis_index("col") * LANES, LANES), LANES)
    total = own_ref[...]
    for ref in (a_ref, b_ref, c_ref):
        part = ref[...].astype(I32).astype(F32)
        total += part * jnp.exp2(-part[CAP - 1 : CAP, :])
    slot = iota((CAP, LANES), 0)
    pick = one_hot(slot == jnp.broadcast_to(rank_ref[0:1, lanes], (CAP, LANES)))
    wide = lax.dot_general(total.astype(BF16), pick, (((0,), (0,)), ((), ())), preferred_element_type=F32)
    same = m_ref[...].astype(F32) == jnp.broadcast_to(occ_ref[0:1, lanes].astype(F32), wide.shape)
    out_ref[...] = jnp.where(same, wide, 0.0).astype(BF16)


def plain_symbols_kernel(
    occ_ref, virt_ref, occ_orbs, k_orbs, m_orbs, own_orbs, occ_out, rank_out, k_out, m_out, own_out, most_out
):
    occ = pack_labels(occ_ref[0:1, :])
    virt = pack_labels(virt_ref[0:7, :])
    first = lax.broadcasted_iota(I32, (LANES, LANES), 0)
    second = lax.broadcasted_iota(I32, (LANES, LANES), 1)
    most = jnp.zeros((1, LANES), I32)
    for start in range(0, occ_orbs.shape[1], LANES):
        sym = pair_symbols(occ, occ_orbs, start)
        occ_out[:, start : start + LANES] = sym
        same = as_column(sym) == jnp.broadcast_to(sym[0:1, :].astype(F32), (LANES, LANES))
        earlier = jnp.where(same & (first < second), 1.0, 0.0)
        rank = jnp.sum(earlier, axis=0, keepdims=True).astype(I32)
        most = jnp.maximum(most, rank)
        rank_out[:, start : start + LANES] = jnp.broadcast_to(rank, (8, LANES))
    most_out[0, 0] = jnp.max(most)
    for start in range(0, k_orbs.shape[1], LANES):
        sym = pair_symbols(virt, k_orbs, start).astype(F32)
        k_out[:, start : start + LANES] = jnp.concatenate([sym, sym], axis=0).astype(BF16)
    for start in range(0, m_orbs.shape[1], LANES):
        m_out[start : start + LANES, :] = as_column(pair_symbols(virt, m_orbs, start)).astype(BF16)
    for start in range(0, own_orbs.shape[1], LANES):
        own_out[start : start + LANES, :] = as_column(pair_symbols(virt, own_orbs, start)).astype(I32)


def plain_compact_kernel(copies, pass_ref, rows_ref, own_ref, occ_ref, rank_ref, out_ref):
    n, pairs = rows_ref.shape
    cols = pairs // LANES
    i = lax.broadcasted_iota(I32, (n, n), 0)
    j = lax.broadcasted_iota(I32, (n, n), 1)
    wanted = ((i >> 1) & 7) * 32 + (i >> 4) * 2 + (i & 1)
    order = jnp.where(j == wanted, 1.0, 0.0).astype(BF16)
    rows = jnp.dot(order, rows_ref[...], preferred_element_type=F32)
    base = pass_ref[0] * CAP
    slot = lax.broadcasted_iota(I32, (CAP, LANES), 0) + base
    own = own_ref[...]
    for c in range(cols):
        lanes = slice(c * LANES, (c + 1) * LANES)
        keep = own == jnp.broadcast_to(occ_ref[0:1, lanes], (n, LANES))
        kept = jnp.where(keep, rows[:, lanes], 0.0).astype(BF16)
        pick = jnp.where(slot == jnp.broadcast_to(rank_ref[0:1, lanes], (CAP, LANES)), 1.0, 0.0).astype(BF16)
        part = lax.dot_general(kept, pick, (((1,), (1,)), ((), ())), preferred_element_type=F32).astype(BF16)
        for r in range(copies):
            out_ref[r, :, c * CAP : (c + 1) * CAP] = part


def plain_product_kernel(core_ref, amp_ref, int_ref, k_ref, m_ref, keep_ref, send_ref, kept):
    depth, width = amp_ref.shape
    block = depth // 16

    @pl.when(pl.program_id(0) == 0)
    def _():
        for r in range(16):
            for source in range(16):
                kept[r * block + source * 16 : r * block + source * 16 + 16, :] = amp_ref[
                    source * block + r * 16 : source * block + r * 16 + 16, :
                ]

    m_sym = m_ref[...]
    chunk = 1024
    total = jnp.zeros((m_ref.shape[0], width), F32)
    for at in range(0, depth, chunk):
        parts = []
        for lane in range(at, at + chunk, LANES):
            lanes = slice(lane, lane + LANES)
            same = m_sym == jnp.broadcast_to(k_ref[0:1, lanes], m_sym.shape)
            parts.append(jnp.where(same, int_ref[:, lanes], jnp.zeros((), BF16)))
        screened = jnp.concatenate(parts, axis=1)
        total += jnp.dot(screened, kept[at : at + chunk, :], preferred_element_type=F32)
    turned = jnp.transpose(total)
    even = core_ref[0] == 0
    for z in range(4):
        low = turned[z * 2 * CAP : z * 2 * CAP + CAP, :]
        high = turned[z * 2 * CAP + CAP : z * 2 * CAP + 2 * CAP, :]
        keep_ref[z] = jnp.where(even, low, high)
        send_ref[z] = jnp.where(even, high, low)


def plain_share_kernel(z_ref, keep_ref, got_ref, *out_refs):
    for step, out_ref in enumerate(out_refs):
        z = (z_ref[0] + step) % 4
        out_ref[...] = keep_ref[z] + got_ref[z]


def plain_expand_kernel(at_ref, a_ref, b_ref, c_ref, d_ref, m_ref, occ_ref, rank_ref, out_ref):
    lanes = pl.ds(pl.multiple_of(at_ref[0] * LANES, LANES), LANES)
    total = (a_ref[...] + b_ref[...] + c_ref[...] + d_ref[...]).astype(BF16)
    slot = lax.broadcasted_iota(I32, (CAP, LANES), 0) + at_ref[1] * CAP
    pick = jnp.where(slot == jnp.broadcast_to(rank_ref[0:1, lanes], (CAP, LANES)), 1.0, 0.0).astype(BF16)
    wide = lax.dot_general(total, pick, (((0,), (0,)), ((), ())), preferred_element_type=F32)
    same = m_ref[...].astype(F32) == jnp.broadcast_to(occ_ref[0:1, lanes].astype(F32), wide.shape)
    out_ref[...] = jnp.where(same, wide, 0.0).astype(BF16)


def params(mib=16):
    return pltpu.CompilerParams(vmem_limit_bytes=mib * 1024 * 1024)


def whole():
    return pl.BlockSpec(memory_space=pltpu.VMEM)


def scalars():
    return pl.BlockSpec(memory_space=pltpu.SMEM)


def plain(amp_store, store_map, integrals, occ_irrep, virt_irrep, occ_orbs, k_orbs, m_orbs):
    rows = lax.axis_size("row")
    cols = lax.axis_size("col")
    stored, pairs = amp_store.shape
    kblock = k_orbs.shape[1]
    m_dev = m_orbs.shape[1]
    my_row = lax.axis_index("row")
    my_col = lax.axis_index("col")
    shape = jax.ShapeDtypeStruct

    place = (store_map // kblock) * (rows * 2) + ((store_map % kblock) // stored) * 2 + store_map % 2
    order = (jnp.arange(stored, dtype=I32)[:, None] == place[None, :]).astype(BF16)
    ordered = jnp.dot(order, amp_store, preferred_element_type=F32).astype(BF16)
    column_rows = lax.all_to_all(ordered, "col", split_axis=0, concat_axis=0, tiled=True)

    own_orbs = lax.dynamic_slice_in_dim(k_orbs.reshape(2, rows, stored), my_row * 16, 16, axis=2).reshape(2, stored)
    occ_lab = jnp.pad(occ_irrep, (0, LANES - occ_irrep.shape[0])).reshape(1, LANES)
    virt_lab = jnp.pad(virt_irrep, (0, 8 * LANES - virt_irrep.shape[0])).reshape(8, LANES)
    occ_sym, rank, k_sym, m_sym, own_sym, most = pl.pallas_call(
        plain_symbols_kernel,
        out_shape=(
            shape((8, pairs), I32),
            shape((8, pairs), I32),
            shape((16, kblock), BF16),
            shape((m_dev, LANES), BF16),
            shape((stored, LANES), I32),
            shape((1, 1), I32),
        ),
        in_specs=[whole()] * 6,
        out_specs=(whole(),) * 5 + (scalars(),),
        compiler_params=params(),
        name="plain_symbols",
    )(occ_lab, virt_lab, occ_orbs, k_orbs, m_orbs, own_orbs)

    def one_pass(step):
        width = cols * CAP
        compact = pl.pallas_call(
            functools.partial(plain_compact_kernel, rows),
            out_shape=shape((rows, stored, width), BF16),
            in_specs=[scalars()] + [whole()] * 4,
            out_specs=whole(),
            compiler_params=params(),
            name="plain_compact",
        )(step.reshape(1), column_rows, own_sym, occ_sym, rank)
        gathered = lax.all_to_all(
            compact.reshape(rows * stored, width), "row", split_axis=0, concat_axis=0, tiled=True
        )
        keep, send = pl.pallas_call(
            plain_product_kernel,
            grid=(m_dev // TM,),
            out_shape=(shape((4, CAP, m_dev), F32),) * 2,
            in_specs=[
                scalars(),
                pl.BlockSpec((kblock, width), lambda i: (0, 0)),
                pl.BlockSpec((TM, kblock), lambda i: (i, 0)),
                pl.BlockSpec((16, kblock), lambda i: (0, 0)),
                pl.BlockSpec((TM, LANES), lambda i: (i, 0)),
            ],
            out_specs=(pl.BlockSpec((4, CAP, TM), lambda i: (0, 0, i)),) * 2,
            scratch_shapes=[pltpu.VMEM((kblock, width), BF16)],
            compiler_params=params(),
            name="plain_product",
        )((my_col % 2).reshape(1), gathered, integrals, k_sym, m_sym)
        got = lax.ppermute(send, "col", [(i, i ^ 1) for i in range(cols)])
        shares = pl.pallas_call(
            plain_share_kernel,
            out_shape=(shape((CAP, m_dev), F32),) * 4,
            in_specs=[scalars(), whole(), whole()],
            out_specs=(whole(),) * 4,
            compiler_params=params(),
            name="plain_share",
        )((my_col // 2).reshape(1), keep, got)
        sums = [shares[0]]
        for distance in range(1, 4):
            hops = [(i, (i + 2 * distance) % cols) for i in range(cols)]
            sums.append(lax.ppermute(shares[distance], "col", hops))
        return pl.pallas_call(
            plain_expand_kernel,
            out_shape=shape((m_dev, LANES), BF16),
            in_specs=[scalars()] + [whole()] * 7,
            out_specs=whole(),
            compiler_params=params(),
            name="plain_expand",
        )(jnp.stack([my_col, step]), *sums, m_sym, occ_sym, rank)

    passes = most[0, 0] // CAP + 1
    return lax.while_loop(
        lambda state: state[0] < passes,
        lambda state: (state[0] + 1, state[1] + one_pass(state[0])),
        (jnp.zeros((), I32), jnp.zeros((m_dev, LANES), BF16)),
    )[1]


def body(amp_store, store_map, integrals, occ_irrep, virt_irrep, occ_orbs, k_orbs, m_orbs):
    rows = lax.axis_size("row")
    cols = lax.axis_size("col")
    stored, pairs = amp_store.shape
    kblock = k_orbs.shape[1]
    m_dev = m_orbs.shape[1]
    shape = jax.ShapeDtypeStruct
    swap = [(i, i ^ 1) for i in range(cols)]
    hops = [[(i, (i + 2 * d) % cols) for i in range(cols)] for d in range(4)]

    def call(kernel, name, out_shape, operands, mib=16, **kw):
        return pl.pallas_call(
            kernel,
            out_shape=out_shape,
            in_specs=[whole()] * len(operands),
            out_specs=kw.pop("out_specs", jax.tree.map(lambda _: whole(), out_shape)),
            compiler_params=params(mib),
            name=name,
            **kw,
        )(*operands)

    own_orbs = lax.dynamic_slice_in_dim(
        k_orbs.reshape(2, rows, stored), lax.axis_index("row") * 16, 16, axis=2
    ).reshape(2, stored)
    other_orbs = lax.ppermute(own_orbs, "col", swap)

    ordered = call(order_kernel, "order", (shape((64, pairs), BF16),) * 4, (store_map.reshape(1, stored), amp_store))
    arrived = [ordered[0]] + [lax.ppermute(ordered[d], "col", hops[d]) for d in range(1, 4)]

    occ_lab = jnp.pad(occ_irrep, (0, LANES - occ_irrep.shape[0])).reshape(1, LANES)
    virt_lab = jnp.pad(virt_irrep, (0, 8 * LANES - virt_irrep.shape[0])).reshape(8, LANES)
    occ_sym, rank, place, spread, k_sym, k_col, m_sym, own_sym, other_sym, bad = call(
        symbols_kernel,
        "symbols",
        (
            shape((8, pairs), I32),
            shape((8, pairs), I32),
            shape((8, pairs), I32),
            shape((8 * BASE, 8 * SPILL), BF16),
            shape((16, kblock), BF16),
            shape((kblock, LANES), BF16),
            shape((m_dev, LANES), BF16),
            shape((LANES, LANES), F32),
            shape((LANES, LANES), F32),
            shape((1, 1), I32),
        ),
        (occ_lab, virt_lab, occ_orbs, k_orbs, m_orbs, own_orbs, other_orbs),
        out_specs=(whole(),) * 9 + (scalars(),),
    )

    mine, theirs = call(
        compact_kernel,
        "compact",
        (shape((PLACES, LANES), BF16),) * 2,
        (*arrived, own_sym, other_sym, occ_sym, place),
    )
    got = lax.ppermute(theirs, "col", swap)
    spreading = jnp.broadcast_to(jnp.concatenate([mine, got], axis=1)[None], (rows, PLACES, stored))
    gathered = lax.all_to_all(spreading, "row", split_axis=0, concat_axis=0, tiled=True)

    keep, send = pl.pallas_call(
        product_kernel,
        grid=(m_dev // 512,),
        out_shape=(shape((4, CAP, m_dev), F32),) * 2,
        in_specs=[
            whole(),
            pl.BlockSpec((512, kblock), lambda i: (i, 0)),
            whole(),
            whole(),
            pl.BlockSpec((512, LANES), lambda i: (i, 0)),
            whole(),
        ],
        out_specs=(pl.BlockSpec((4, CAP, 512), lambda i: (0, 0, i)),) * 2,
        scratch_shapes=[pltpu.VMEM((kblock, 256), BF16)],
        compiler_params=params(24),
        name="product",
    )(gathered, integrals, k_sym, k_col, m_sym, spread)
    partner = lax.ppermute(send, "col", swap)
    shares = call(
        share_kernel,
        "share",
        (shape((CAP, m_dev), F32),) + (shape((CAP, m_dev), jnp.int16),) * 3,
        (keep, partner),
    )
    sums = [shares[0]] + [lax.ppermute(shares[d], "col", hops[d]) for d in range(1, 4)]
    result = call(expand_kernel, "expand", shape((m_dev, LANES), BF16), (*sums, m_sym, occ_sym, rank))

    return lax.while_loop(
        lambda state: state[0] > 0,
        lambda state: (
            jnp.zeros((), I32),
            plain(amp_store, store_map, integrals, occ_irrep, virt_irrep, occ_orbs, k_orbs, m_orbs),
        ),
        (bad[0, 0], result),
    )[1]


def solution(mesh):
    in_specs = (
        P(("row", "col"), None),
        P(("row", "col")),
        P("row", "col"),
        P(),
        P(),
        P(),
        P(None, "col"),
        P(None, "row"),
    )
    out_specs = P("row", "col")
    return jax.shard_map(body, mesh=mesh, in_specs=in_specs, out_specs=out_specs, check_vma=False)
```

```python
import functools

import jax
import jax.numpy as jnp
from jax import lax
from jax.experimental import pallas as pl
from jax.experimental.pallas import tpu as pltpu
from jax.sharding import PartitionSpec as P

BF16 = jnp.bfloat16
F32 = jnp.float32
I32 = jnp.int32
LANES = 128
CAP = 32
BASE = 16
SPILL = 48
PLACES = 8 * BASE + SPILL
TM = 256
ROOM = 64
TILE = 1024


def pack_labels(labels):
    word = labels[0:1, :]
    for i in range(1, labels.shape[0]):
        word = word | (labels[i : i + 1, :] << (4 * i))
    return jnp.broadcast_to(word, (8, LANES))


def look_up(packed, orbitals):
    orbitals = jnp.broadcast_to(orbitals, (8, LANES))
    word = jnp.take_along_axis(packed, orbitals & (LANES - 1), axis=1)
    return (word >> ((orbitals >> 7) << 2)) & 7


def pair_symbols(packed, orbs_ref, start):
    lanes = slice(start, start + LANES)
    return look_up(packed, orbs_ref[0:1, lanes]) ^ look_up(packed, orbs_ref[1:2, lanes])


def as_column(symbols):
    row = jnp.broadcast_to(symbols[0:1, :].astype(F32), (LANES, LANES))
    return jnp.transpose(row)


def one_hot(mask):
    return jnp.where(mask, 1.0, 0.0).astype(BF16)


def rows_dot(a, b):
    return lax.dot_general(a, b, (((1,), (1,)), ((), ())), preferred_element_type=F32)


def iota(shape, axis):
    return lax.broadcasted_iota(I32, shape, axis)


def order_kernel(map_ref, amp_ref, *out_refs):
    z, core = lax.axis_index("col") >> 1, lax.axis_index("col") & 1
    k = map_ref[...]
    col, row, within = k >> 12, (k >> 8) & 15, k & 1
    place = ((((col >> 1) - z) & 3) * 2 + ((col & 1) ^ core)) * 32 + row * 2 + within
    n = amp_ref.shape[0]
    order = one_hot(iota((n, n), 0) == jnp.broadcast_to(place, (n, n)))
    rows = jnp.dot(order, amp_ref[...], preferred_element_type=F32).astype(BF16)
    for d, out_ref in enumerate(out_refs):
        out_ref[...] = rows[d * 64 : d * 64 + 64, :]


def symbols_kernel(
    occ_ref, virt_ref, occ_orbs, k_orbs, m_orbs, own_orbs, other_orbs,
    occ_out, rank_out, place_out, spread_out, k_out, k_col_out, m_out, own_out, other_out, bad_out,
):
    core = lax.axis_index("col") & 1
    occ = pack_labels(occ_ref[0:1, :])
    virt = pack_labels(virt_ref[0:7, :])
    first = iota((LANES, LANES), 0)
    second = iota((LANES, LANES), 1)
    group = iota((8, LANES), 0)
    used = jnp.zeros((8, 1), I32)
    bad = jnp.zeros((1, LANES), I32)
    for c in range(occ_orbs.shape[1] // LANES):
        lanes = slice(c * LANES, (c + 1) * LANES)
        sym = pair_symbols(occ, occ_orbs, c * LANES)
        occ_out[:, lanes] = sym
        same = as_column(sym) == jnp.broadcast_to(sym[0:1, :].astype(F32), (LANES, LANES))
        rank = jnp.sum(jnp.where(same & (first < second), 1.0, 0.0), axis=0, keepdims=True).astype(I32)
        rank_out[:, lanes] = jnp.broadcast_to(rank, (8, LANES))
        mine = sym == group
        extra = jnp.sum(jnp.where(mine, used, 0), axis=0, keepdims=True) + rank - BASE
        used = used + jnp.maximum(jnp.sum(jnp.where(mine, 1, 0), axis=1, keepdims=True) - BASE, 0)
        spilt = rank >= BASE
        bad = jnp.maximum(bad, jnp.where(spilt & ((extra >= SPILL) | (rank >= CAP - 1)), 1, 0))
        fits = spilt & (extra < SPILL)
        place = jnp.where(spilt, jnp.where(fits, 8 * BASE + extra, -1), c * BASE + rank)
        place_out[:, lanes] = jnp.broadcast_to(place, (8, LANES))
        at = jnp.where(spilt, rank - BASE, -1)
        entry = jnp.where(fits, sym[0:1, :] * ROOM + extra, -1)
        to = one_hot(iota((BASE, LANES), 0) == jnp.broadcast_to(at, (BASE, LANES)))
        source = one_hot(iota((8 * ROOM, LANES), 0) == jnp.broadcast_to(entry, (8 * ROOM, LANES)))
        spread_out[c * BASE : (c + 1) * BASE, :] = rows_dot(to, source).astype(BF16)
    bad_out[0, 0] = jnp.max(bad)
    for start in range(0, k_orbs.shape[1], LANES):
        sym = pair_symbols(virt, k_orbs, start)
        wide = sym.astype(F32)
        k_out[:, start : start + LANES] = jnp.concatenate([wide, wide], axis=0).astype(BF16)
        k_col_out[start : start + LANES, :] = as_column(sym).astype(BF16)
    for start in range(0, m_orbs.shape[1], LANES):
        m_out[start : start + LANES, :] = as_column(pair_symbols(virt, m_orbs, start)).astype(BF16)
    i, j = iota((LANES, 2 * LANES), 0), iota((LANES, 2 * LANES), 1)
    pick = one_hot(j == (i >> 1) * 4 + core * 2 + (i & 1))
    for orbs, out in ((own_orbs, own_out), (other_orbs, other_out)):
        column = jnp.concatenate([as_column(pair_symbols(virt, orbs, s)) for s in (0, LANES)], axis=0)
        out[...] = jnp.dot(pick, column.astype(BF16), preferred_element_type=F32)


def compact_kernel(a_ref, b_ref, c_ref, d_ref, own_ref, other_ref, occ_ref, place_ref, mine_out, theirs_out):
    z = lax.axis_index("col") >> 1
    rows = jnp.concatenate([a_ref[...], b_ref[...], c_ref[...], d_ref[...]], axis=0)
    pairs = rows.shape[1]
    squeeze = one_hot(iota((PLACES, pairs), 0) == jnp.broadcast_to(place_ref[0:1, :], (PLACES, pairs)))
    occ = jnp.broadcast_to(occ_ref[0:1, :].astype(F32), (LANES, pairs))
    i, j = iota((LANES, 2 * LANES), 0), iota((LANES, 2 * LANES), 1)
    row, source, within = i >> 3, (i >> 1) & 3, i & 1
    for side, sym_ref, out in ((0, own_ref, mine_out), (1, other_ref, theirs_out)):
        order = one_hot(j == (((z - source) & 3) * 2 + side) * 32 + row * 2 + within)
        turned = jnp.dot(order, rows, preferred_element_type=F32)
        sym = jnp.concatenate([sym_ref[...]] * (pairs // LANES), axis=1)
        kept = jnp.where(sym == occ, turned, 0.0).astype(BF16)
        out[...] = rows_dot(squeeze, kept).astype(BF16)


def product_kernel(amp_ref, int_ref, k_ref, k_col_ref, m_ref, spread_ref, keep_ref, send_ref, kept, local, sems):
    core = lax.axis_index("col") & 1
    depth = k_ref.shape[1]
    tiles = int_ref.shape[0] // TILE

    def fetch(n):
        rows = pl.ds(pl.multiple_of(n * TILE, TILE), TILE)
        return pltpu.make_async_copy(int_ref.at[rows], local.at[rows], sems.at[n])

    def begin(n, carry):
        fetch(n).start()
        return carry

    lax.fori_loop(0, tiles, begin, 0)

    i, j = iota((256, 256), 0), iota((256, 256), 1)
    order = one_hot(j == (((i >> 1) & 1) ^ core) * 128 + (i >> 4) * 8 + ((i >> 2) & 3) * 2 + (i & 1))
    spread = spread_ref[...]
    nought = jnp.zeros((), BF16)
    gap = jnp.zeros((ROOM - SPILL, 256), BF16)
    second = iota((16, LANES), 1) >= ROOM
    groups = [
        jnp.broadcast_to(jnp.where(second, 2.0 * t + 1.0, 2.0 * t).astype(BF16)[0:1, :], (256, LANES))
        for t in range(4)
    ]

    def unpack(source, carry):
        slots = amp_ref[source]
        stack = jnp.concatenate([slots, gap, slots[8 * BASE :], gap], axis=0)
        block = rows_dot(order, stack).astype(BF16)
        at = [pl.ds(pl.multiple_of(r * 256 + source * 16, 16), 16) for r in range(16)]
        sym = jnp.concatenate([k_col_ref[rows, :] for rows in at], axis=0)
        shared = [jnp.where(sym == group, block[:, 8 * BASE :], nought) for group in groups]
        spilt = rows_dot(jnp.concatenate(shared, axis=1), spread).astype(BF16)
        for r, rows in enumerate(at):
            kept[rows, : 8 * BASE] = block[r * 16 : r * 16 + 16, : 8 * BASE]
            kept[rows, 8 * BASE :] = spilt[r * 16 : r * 16 + 16, :]
        return carry

    lax.fori_loop(0, 16, unpack, 0, unroll=8)

    even = core == 0
    chunk = 1024

    def multiply(n, carry):
        rows = pl.ds(pl.multiple_of(n * TILE, TILE), TILE)
        fetch(n).wait()
        m_sym = m_ref[rows, :]
        total = jnp.zeros((TILE, 256), F32)
        for at in range(0, depth, chunk):
            parts = []
            for start in range(at, at + chunk, LANES):
                lanes = slice(start, start + LANES)
                same = m_sym == jnp.broadcast_to(k_ref[0:1, lanes], m_sym.shape)
                parts.append(jnp.where(same, local[rows, lanes], nought))
            screened = jnp.concatenate(parts, axis=1)
            total += jnp.dot(screened, kept[at : at + chunk, :], preferred_element_type=F32)
        turned = jnp.transpose(total)
        for z in range(4):
            for half in range(2):
                at = half * 128 + z * 2 * BASE
                low, high = turned[at : at + BASE, :], turned[at + BASE : at + 2 * BASE, :]
                slots = slice(half * BASE, half * BASE + BASE)
                keep_ref[z, slots, rows] = jnp.where(even, low, high)
                send_ref[z, slots, rows] = jnp.where(even, high, low)
        return carry

    lax.fori_loop(0, tiles, multiply, 0)


def share_kernel(keep_ref, got_ref, own_ref, *out_refs):
    z = lax.axis_index("col") >> 1
    own_ref[...] = keep_ref[z] + got_ref[z]
    for step, out_ref in enumerate(out_refs):
        there = (z + step + 1) & 3
        total = keep_ref[there] + got_ref[there]
        largest = jnp.max(jnp.abs(total), axis=0, keepdims=True)
        power = jnp.minimum(jnp.floor(14.9 - jnp.log2(jnp.maximum(largest, 1e-37))), 120.0)
        scaled = total * jnp.exp2(power)
        scaled = jnp.where(iota(total.shape, 0) == CAP - 1, power, scaled)
        out_ref[...] = (scaled + jnp.where(scaled >= 0, 0.5, -0.5)).astype(I32).astype(jnp.int16)


def expand_kernel(own_ref, a_ref, b_ref, c_ref, m_ref, occ_ref, rank_ref, out_ref):
    lanes = pl.ds(pl.multiple_of(lax.axis_index("col") * LANES, LANES), LANES)
    total = own_ref[...]
    for ref in (a_ref, b_ref, c_ref):
        part = ref[...].astype(I32).astype(F32)
        total += part * jnp.exp2(-part[CAP - 1 : CAP, :])
    slot = iota((CAP, LANES), 0)
    pick = one_hot(slot == jnp.broadcast_to(rank_ref[0:1, lanes], (CAP, LANES)))
    wide = lax.dot_general(total.astype(BF16), pick, (((0,), (0,)), ((), ())), preferred_element_type=F32)
    same = m_ref[...].astype(F32) == jnp.broadcast_to(occ_ref[0:1, lanes].astype(F32), wide.shape)
    out_ref[...] = jnp.where(same, wide, 0.0).astype(BF16)


def plain_symbols_kernel(
    occ_ref, virt_ref, occ_orbs, k_orbs, m_orbs, own_orbs, occ_out, rank_out, k_out, m_out, own_out, most_out
):
    occ = pack_labels(occ_ref[0:1, :])
    virt = pack_labels(virt_ref[0:7, :])
    first = lax.broadcasted_iota(I32, (LANES, LANES), 0)
    second = lax.broadcasted_iota(I32, (LANES, LANES), 1)
    most = jnp.zeros((1, LANES), I32)
    for start in range(0, occ_orbs.shape[1], LANES):
        sym = pair_symbols(occ, occ_orbs, start)
        occ_out[:, start : start + LANES] = sym
        same = as_column(sym) == jnp.broadcast_to(sym[0:1, :].astype(F32), (LANES, LANES))
        earlier = jnp.where(same & (first < second), 1.0, 0.0)
        rank = jnp.sum(earlier, axis=0, keepdims=True).astype(I32)
        most = jnp.maximum(most, rank)
        rank_out[:, start : start + LANES] = jnp.broadcast_to(rank, (8, LANES))
    most_out[0, 0] = jnp.max(most)
    for start in range(0, k_orbs.shape[1], LANES):
        sym = pair_symbols(virt, k_orbs, start).astype(F32)
        k_out[:, start : start + LANES] = jnp.concatenate([sym, sym], axis=0).astype(BF16)
    for start in range(0, m_orbs.shape[1], LANES):
        m_out[start : start + LANES, :] = as_column(pair_symbols(virt, m_orbs, start)).astype(BF16)
    for start in range(0, own_orbs.shape[1], LANES):
        own_out[start : start + LANES, :] = as_column(pair_symbols(virt, own_orbs, start)).astype(I32)


def plain_compact_kernel(copies, pass_ref, rows_ref, own_ref, occ_ref, rank_ref, out_ref):
    n, pairs = rows_ref.shape
    cols = pairs // LANES
    i = lax.broadcasted_iota(I32, (n, n), 0)
    j = lax.broadcasted_iota(I32, (n, n), 1)
    wanted = ((i >> 1) & 7) * 32 + (i >> 4) * 2 + (i & 1)
    order = jnp.where(j == wanted, 1.0, 0.0).astype(BF16)
    rows = jnp.dot(order, rows_ref[...], preferred_element_type=F32)
    base = pass_ref[0] * CAP
    slot = lax.broadcasted_iota(I32, (CAP, LANES), 0) + base
    own = own_ref[...]
    for c in range(cols):
        lanes = slice(c * LANES, (c + 1) * LANES)
        keep = own == jnp.broadcast_to(occ_ref[0:1, lanes], (n, LANES))
        kept = jnp.where(keep, rows[:, lanes], 0.0).astype(BF16)
        pick = jnp.where(slot == jnp.broadcast_to(rank_ref[0:1, lanes], (CAP, LANES)), 1.0, 0.0).astype(BF16)
        part = lax.dot_general(kept, pick, (((1,), (1,)), ((), ())), preferred_element_type=F32).astype(BF16)
        for r in range(copies):
            out_ref[r, :, c * CAP : (c + 1) * CAP] = part


def plain_product_kernel(core_ref, amp_ref, int_ref, k_ref, m_ref, keep_ref, send_ref, kept):
    depth, width = amp_ref.shape
    block = depth // 16

    @pl.when(pl.program_id(0) == 0)
    def _():
        for r in range(16):
            for source in range(16):
                kept[r * block + source * 16 : r * block + source * 16 + 16, :] = amp_ref[
                    source * block + r * 16 : source * block + r * 16 + 16, :
                ]

    m_sym = m_ref[...]
    chunk = 1024
    total = jnp.zeros((m_ref.shape[0], width), F32)
    for at in range(0, depth, chunk):
        parts = []
        for lane in range(at, at + chunk, LANES):
            lanes = slice(lane, lane + LANES)
            same = m_sym == jnp.broadcast_to(k_ref[0:1, lanes], m_sym.shape)
            parts.append(jnp.where(same, int_ref[:, lanes], jnp.zeros((), BF16)))
        screened = jnp.concatenate(parts, axis=1)
        total += jnp.dot(screened, kept[at : at + chunk, :], preferred_element_type=F32)
    turned = jnp.transpose(total)
    even = core_ref[0] == 0
    for z in range(4):
        low = turned[z * 2 * CAP : z * 2 * CAP + CAP, :]
        high = turned[z * 2 * CAP + CAP : z * 2 * CAP + 2 * CAP, :]
        keep_ref[z] = jnp.where(even, low, high)
        send_ref[z] = jnp.where(even, high, low)


def plain_share_kernel(z_ref, keep_ref, got_ref, *out_refs):
    for step, out_ref in enumerate(out_refs):
        z = (z_ref[0] + step) % 4
        out_ref[...] = keep_ref[z] + got_ref[z]


def plain_expand_kernel(at_ref, a_ref, b_ref, c_ref, d_ref, m_ref, occ_ref, rank_ref, out_ref):
    lanes = pl.ds(pl.multiple_of(at_ref[0] * LANES, LANES), LANES)
    total = (a_ref[...] + b_ref[...] + c_ref[...] + d_ref[...]).astype(BF16)
    slot = lax.broadcasted_iota(I32, (CAP, LANES), 0) + at_ref[1] * CAP
    pick = jnp.where(slot == jnp.broadcast_to(rank_ref[0:1, lanes], (CAP, LANES)), 1.0, 0.0).astype(BF16)
    wide = lax.dot_general(total, pick, (((0,), (0,)), ((), ())), preferred_element_type=F32)
    same = m_ref[...].astype(F32) == jnp.broadcast_to(occ_ref[0:1, lanes].astype(F32), wide.shape)
    out_ref[...] = jnp.where(same, wide, 0.0).astype(BF16)


def params(mib=16):
    return pltpu.CompilerParams(vmem_limit_bytes=mib * 1024 * 1024)


def whole():
    return pl.BlockSpec(memory_space=pltpu.VMEM)


def scalars():
    return pl.BlockSpec(memory_space=pltpu.SMEM)


def plain(amp_store, store_map, integrals, occ_irrep, virt_irrep, occ_orbs, k_orbs, m_orbs):
    rows = lax.axis_size("row")
    cols = lax.axis_size("col")
    stored, pairs = amp_store.shape
    kblock = k_orbs.shape[1]
    m_dev = m_orbs.shape[1]
    my_row = lax.axis_index("row")
    my_col = lax.axis_index("col")
    shape = jax.ShapeDtypeStruct

    place = (store_map // kblock) * (rows * 2) + ((store_map % kblock) // stored) * 2 + store_map % 2
    order = (jnp.arange(stored, dtype=I32)[:, None] == place[None, :]).astype(BF16)
    ordered = jnp.dot(order, amp_store, preferred_element_type=F32).astype(BF16)
    column_rows = lax.all_to_all(ordered, "col", split_axis=0, concat_axis=0, tiled=True)

    own_orbs = lax.dynamic_slice_in_dim(k_orbs.reshape(2, rows, stored), my_row * 16, 16, axis=2).reshape(2, stored)
    occ_lab = jnp.pad(occ_irrep, (0, LANES - occ_irrep.shape[0])).reshape(1, LANES)
    virt_lab = jnp.pad(virt_irrep, (0, 8 * LANES - virt_irrep.shape[0])).reshape(8, LANES)
    occ_sym, rank, k_sym, m_sym, own_sym, most = pl.pallas_call(
        plain_symbols_kernel,
        out_shape=(
            shape((8, pairs), I32),
            shape((8, pairs), I32),
            shape((16, kblock), BF16),
            shape((m_dev, LANES), BF16),
            shape((stored, LANES), I32),
            shape((1, 1), I32),
        ),
        in_specs=[whole()] * 6,
        out_specs=(whole(),) * 5 + (scalars(),),
        compiler_params=params(),
        name="plain_symbols",
    )(occ_lab, virt_lab, occ_orbs, k_orbs, m_orbs, own_orbs)

    def one_pass(step):
        width = cols * CAP
        compact = pl.pallas_call(
            functools.partial(plain_compact_kernel, rows),
            out_shape=shape((rows, stored, width), BF16),
            in_specs=[scalars()] + [whole()] * 4,
            out_specs=whole(),
            compiler_params=params(),
            name="plain_compact",
        )(step.reshape(1), column_rows, own_sym, occ_sym, rank)
        gathered = lax.all_to_all(
            compact.reshape(rows * stored, width), "row", split_axis=0, concat_axis=0, tiled=True
        )
        keep, send = pl.pallas_call(
            plain_product_kernel,
            grid=(m_dev // TM,),
            out_shape=(shape((4, CAP, m_dev), F32),) * 2,
            in_specs=[
                scalars(),
                pl.BlockSpec((kblock, width), lambda i: (0, 0)),
                pl.BlockSpec((TM, kblock), lambda i: (i, 0)),
                pl.BlockSpec((16, kblock), lambda i: (0, 0)),
                pl.BlockSpec((TM, LANES), lambda i: (i, 0)),
            ],
            out_specs=(pl.BlockSpec((4, CAP, TM), lambda i: (0, 0, i)),) * 2,
            scratch_shapes=[pltpu.VMEM((kblock, width), BF16)],
            compiler_params=params(),
            name="plain_product",
        )((my_col % 2).reshape(1), gathered, integrals, k_sym, m_sym)
        got = lax.ppermute(send, "col", [(i, i ^ 1) for i in range(cols)])
        shares = pl.pallas_call(
            plain_share_kernel,
            out_shape=(shape((CAP, m_dev), F32),) * 4,
            in_specs=[scalars(), whole(), whole()],
            out_specs=(whole(),) * 4,
            compiler_params=params(),
            name="plain_share",
        )((my_col // 2).reshape(1), keep, got)
        sums = [shares[0]]
        for distance in range(1, 4):
            hops = [(i, (i + 2 * distance) % cols) for i in range(cols)]
            sums.append(lax.ppermute(shares[distance], "col", hops))
        return pl.pallas_call(
            plain_expand_kernel,
            out_shape=shape((m_dev, LANES), BF16),
            in_specs=[scalars()] + [whole()] * 7,
            out_specs=whole(),
            compiler_params=params(),
            name="plain_expand",
        )(jnp.stack([my_col, step]), *sums, m_sym, occ_sym, rank)

    passes = most[0, 0] // CAP + 1
    return lax.while_loop(
        lambda state: state[0] < passes,
        lambda state: (state[0] + 1, state[1] + one_pass(state[0])),
        (jnp.zeros((), I32), jnp.zeros((m_dev, LANES), BF16)),
    )[1]


def body(amp_store, store_map, integrals, occ_irrep, virt_irrep, occ_orbs, k_orbs, m_orbs):
    rows = lax.axis_size("row")
    cols = lax.axis_size("col")
    stored, pairs = amp_store.shape
    kblock = k_orbs.shape[1]
    m_dev = m_orbs.shape[1]
    shape = jax.ShapeDtypeStruct
    swap = [(i, i ^ 1) for i in range(cols)]
    hops = [[(i, (i + 2 * d) % cols) for i in range(cols)] for d in range(4)]

    def call(kernel, name, out_shape, operands, mib=16, **kw):
        return pl.pallas_call(
            kernel,
            out_shape=out_shape,
            in_specs=kw.pop("in_specs", [whole()] * len(operands)),
            out_specs=kw.pop("out_specs", jax.tree.map(lambda _: whole(), out_shape)),
            compiler_params=params(mib),
            name=name,
            **kw,
        )(*operands)

    own_orbs = lax.dynamic_slice_in_dim(
        k_orbs.reshape(2, rows, stored), lax.axis_index("row") * 16, 16, axis=2
    ).reshape(2, stored)
    other_orbs = lax.ppermute(own_orbs, "col", swap)

    ordered = call(order_kernel, "order", (shape((64, pairs), BF16),) * 4, (store_map.reshape(1, stored), amp_store))
    arrived = [ordered[0]] + [lax.ppermute(ordered[d], "col", hops[d]) for d in range(1, 4)]

    occ_lab = jnp.pad(occ_irrep, (0, LANES - occ_irrep.shape[0])).reshape(1, LANES)
    virt_lab = jnp.pad(virt_irrep, (0, 8 * LANES - virt_irrep.shape[0])).reshape(8, LANES)
    occ_sym, rank, place, spread, k_sym, k_col, m_sym, own_sym, other_sym, bad = call(
        symbols_kernel,
        "symbols",
        (
            shape((8, pairs), I32),
            shape((8, pairs), I32),
            shape((8, pairs), I32),
            shape((8 * BASE, 8 * ROOM), BF16),
            shape((16, kblock), BF16),
            shape((kblock, LANES), BF16),
            shape((m_dev, LANES), BF16),
            shape((LANES, LANES), F32),
            shape((LANES, LANES), F32),
            shape((1, 1), I32),
        ),
        (occ_lab, virt_lab, occ_orbs, k_orbs, m_orbs, own_orbs, other_orbs),
        out_specs=(whole(),) * 9 + (scalars(),),
    )

    mine, theirs = call(
        compact_kernel,
        "compact",
        (shape((PLACES, LANES), BF16),) * 2,
        (*arrived, own_sym, other_sym, occ_sym, place),
    )
    got = lax.ppermute(theirs, "col", swap)
    spreading = jnp.broadcast_to(jnp.concatenate([mine, got], axis=1)[None], (rows, PLACES, stored))
    gathered = lax.all_to_all(spreading, "row", split_axis=0, concat_axis=0, tiled=True)

    keep, send = call(
        product_kernel,
        "product",
        (shape((4, CAP, m_dev), F32),) * 2,
        (gathered, integrals, k_sym, k_col, m_sym, spread),
        30,
        in_specs=[whole(), pl.BlockSpec(memory_space=pl.ANY)] + [whole()] * 4,
        scratch_shapes=[
            pltpu.VMEM((kblock, 256), BF16),
            pltpu.VMEM((m_dev, kblock), BF16),
            pltpu.SemaphoreType.DMA((m_dev // TILE,)),
        ],
    )
    partner = lax.ppermute(send, "col", swap)
    shares = call(
        share_kernel,
        "share",
        (shape((CAP, m_dev), F32),) + (shape((CAP, m_dev), jnp.int16),) * 3,
        (keep, partner),
    )
    sums = [shares[0]] + [lax.ppermute(shares[d], "col", hops[d]) for d in range(1, 4)]
    result = call(expand_kernel, "expand", shape((m_dev, LANES), BF16), (*sums, m_sym, occ_sym, rank))

    return lax.while_loop(
        lambda state: state[0] > 0,
        lambda state: (
            jnp.zeros((), I32),
            plain(amp_store, store_map, integrals, occ_irrep, virt_irrep, occ_orbs, k_orbs, m_orbs),
        ),
        (bad[0, 0], result),
    )[1]


def solution(mesh):
    in_specs = (
        P(("row", "col"), None),
        P(("row", "col")),
        P("row", "col"),
        P(),
        P(),
        P(),
        P(None, "col"),
        P(None, "row"),
    )
    out_specs = P("row", "col")
    return jax.shard_map(body, mesh=mesh, in_specs=in_specs, out_specs=out_specs, check_vma=False)
```

```python
import functools

import jax
import jax.numpy as jnp
from jax import lax
from jax.experimental import pallas as pl
from jax.experimental.pallas import tpu as pltpu
from jax.sharding import PartitionSpec as P

BF16 = jnp.bfloat16
F32 = jnp.float32
I32 = jnp.int32
LANES = 128
CAP = 32
BASE = 16
SPILL = 48
PLACES = 8 * BASE + SPILL
TM = 256
ROOM = 64
TILE = 1024


def pack_labels(labels):
    word = labels[0:1, :]
    for i in range(1, labels.shape[0]):
        word = word | (labels[i : i + 1, :] << (4 * i))
    return jnp.broadcast_to(word, (8, LANES))


def look_up(packed, orbitals):
    orbitals = jnp.broadcast_to(orbitals, (8, LANES))
    word = jnp.take_along_axis(packed, orbitals & (LANES - 1), axis=1)
    return (word >> ((orbitals >> 7) << 2)) & 7


def pair_symbols(packed, orbs_ref, start):
    lanes = slice(start, start + LANES)
    return look_up(packed, orbs_ref[0:1, lanes]) ^ look_up(packed, orbs_ref[1:2, lanes])


def as_column(symbols):
    row = jnp.broadcast_to(symbols[0:1, :].astype(F32), (LANES, LANES))
    return jnp.transpose(row)


def one_hot(mask):
    return jnp.where(mask, 1.0, 0.0).astype(BF16)


def rows_dot(a, b):
    return lax.dot_general(a, b, (((1,), (1,)), ((), ())), preferred_element_type=F32)


def iota(shape, axis):
    return lax.broadcasted_iota(I32, shape, axis)


def order_kernel(map_ref, amp_ref, *out_refs):
    z, core = lax.axis_index("col") >> 1, lax.axis_index("col") & 1
    k = map_ref[...]
    col, row, within = k >> 12, (k >> 8) & 15, k & 1
    place = ((((col >> 1) - z) & 3) * 2 + ((col & 1) ^ core)) * 32 + row * 2 + within
    n = amp_ref.shape[0]
    order = one_hot(iota((n, n), 0) == jnp.broadcast_to(place, (n, n)))
    rows = jnp.dot(order, amp_ref[...], preferred_element_type=F32).astype(BF16)
    for d, out_ref in enumerate(out_refs):
        out_ref[...] = rows[d * 64 : d * 64 + 64, :]


def symbols_kernel(
    occ_ref, virt_ref, occ_orbs, k_orbs, m_orbs, other_orbs,
    occ_out, rank_out, place_out, spread_out, k_out, k_col_out, m_out, own_out, other_out, bad_out, other_col,
):
    core = lax.axis_index("col") & 1
    occ = pack_labels(occ_ref[0:1, :])
    virt = pack_labels(virt_ref[0:7, :])
    first = iota((LANES, LANES), 0)
    second = iota((LANES, LANES), 1)
    group = iota((8, LANES), 0)
    used = jnp.zeros((8, 1), I32)
    bad = jnp.zeros((1, LANES), I32)
    for c in range(occ_orbs.shape[1] // LANES):
        lanes = slice(c * LANES, (c + 1) * LANES)
        sym = pair_symbols(occ, occ_orbs, c * LANES)
        occ_out[:, lanes] = sym
        same = as_column(sym) == jnp.broadcast_to(sym[0:1, :].astype(F32), (LANES, LANES))
        rank = jnp.sum(jnp.where(same & (first < second), 1.0, 0.0), axis=0, keepdims=True).astype(I32)
        rank_out[:, lanes] = jnp.broadcast_to(rank, (8, LANES))
        mine = sym == group
        extra = jnp.sum(jnp.where(mine, used, 0), axis=0, keepdims=True) + rank - BASE
        used = used + jnp.maximum(jnp.sum(jnp.where(mine, 1, 0), axis=1, keepdims=True) - BASE, 0)
        spilt = rank >= BASE
        bad = jnp.maximum(bad, jnp.where(spilt & ((extra >= SPILL) | (rank >= CAP - 1)), 1, 0))
        fits = spilt & (extra < SPILL)
        place = jnp.where(spilt, jnp.where(fits, 8 * BASE + extra, -1), c * BASE + rank)
        place_out[:, lanes] = jnp.broadcast_to(place, (8, LANES))
        at = jnp.where(spilt, rank - BASE, -1)
        entry = jnp.where(fits, sym[0:1, :] * ROOM + extra, -1)
        to = one_hot(iota((BASE, LANES), 0) == jnp.broadcast_to(at, (BASE, LANES)))
        source = one_hot(iota((8 * ROOM, LANES), 0) == jnp.broadcast_to(entry, (8 * ROOM, LANES)))
        spread_out[c * BASE : (c + 1) * BASE, :] = rows_dot(to, source).astype(BF16)
    bad_out[0, 0] = jnp.max(bad)
    for start in range(0, k_orbs.shape[1], LANES):
        sym = pair_symbols(virt, k_orbs, start)
        wide = sym.astype(F32)
        k_out[:, start : start + LANES] = jnp.concatenate([wide, wide], axis=0).astype(BF16)
        k_col_out[start : start + LANES, :] = as_column(sym).astype(BF16)
        other_col[start : start + LANES, :] = as_column(pair_symbols(virt, other_orbs, start)).astype(BF16)
    for start in range(0, m_orbs.shape[1], LANES):
        m_out[start : start + LANES, :] = as_column(pair_symbols(virt, m_orbs, start)).astype(BF16)
    i, j = iota((LANES, 2 * LANES), 0), iota((LANES, 2 * LANES), 1)
    pick = one_hot(j == (i >> 1) * 4 + core * 2 + (i & 1))
    mine = pl.multiple_of(lax.axis_index("row") * 16, 16)
    for ref, out in ((k_col_out, own_out), (other_col, other_out)):
        column = jnp.concatenate([ref[pl.ds(r * 256 + mine, 16), :] for r in range(16)], axis=0)
        out[...] = jnp.dot(pick, column, preferred_element_type=F32)


def compact_kernel(a_ref, b_ref, c_ref, d_ref, own_ref, other_ref, occ_ref, place_ref, mine_out, theirs_out):
    z = lax.axis_index("col") >> 1
    rows = jnp.concatenate([a_ref[...], b_ref[...], c_ref[...], d_ref[...]], axis=0)
    pairs = rows.shape[1]
    squeeze = one_hot(iota((PLACES, pairs), 0) == jnp.broadcast_to(place_ref[0:1, :], (PLACES, pairs)))
    occ = jnp.broadcast_to(occ_ref[0:1, :].astype(F32), (LANES, pairs))
    i, j = iota((LANES, 2 * LANES), 0), iota((LANES, 2 * LANES), 1)
    row, source, within = i >> 3, (i >> 1) & 3, i & 1
    for side, sym_ref, out in ((0, own_ref, mine_out), (1, other_ref, theirs_out)):
        order = one_hot(j == (((z - source) & 3) * 2 + side) * 32 + row * 2 + within)
        turned = jnp.dot(order, rows, preferred_element_type=F32)
        sym = jnp.concatenate([sym_ref[...]] * (pairs // LANES), axis=1)
        kept = jnp.where(sym == occ, turned, 0.0).astype(BF16)
        out[...] = rows_dot(squeeze, kept).astype(BF16)


def product_kernel(amp_ref, int_ref, k_ref, k_col_ref, m_ref, spread_ref, keep_ref, send_ref, kept, local, sems):
    core = lax.axis_index("col") & 1
    depth = k_ref.shape[1]
    tiles = int_ref.shape[0] // TILE

    def fetch(n):
        rows = pl.ds(pl.multiple_of(n * TILE, TILE), TILE)
        return pltpu.make_async_copy(int_ref.at[rows], local.at[rows], sems.at[n])

    def begin(n, carry):
        fetch(n).start()
        return carry

    lax.fori_loop(0, tiles, begin, 0)

    i, j = iota((256, 256), 0), iota((256, 256), 1)
    order = one_hot(j == (((i >> 1) & 1) ^ core) * 128 + (i >> 4) * 8 + ((i >> 2) & 3) * 2 + (i & 1))
    spread = spread_ref[...]
    nought = jnp.zeros((), BF16)
    gap = jnp.zeros((ROOM - SPILL, 256), BF16)
    second = iota((16, LANES), 1) >= ROOM
    groups = [
        jnp.broadcast_to(jnp.where(second, 2.0 * t + 1.0, 2.0 * t).astype(BF16)[0:1, :], (256, LANES))
        for t in range(4)
    ]

    def unpack(source, carry):
        slots = amp_ref[source]
        stack = jnp.concatenate([slots, gap, slots[8 * BASE :], gap], axis=0)
        block = rows_dot(order, stack).astype(BF16)
        at = [pl.ds(pl.multiple_of(r * 256 + source * 16, 16), 16) for r in range(16)]
        sym = jnp.concatenate([k_col_ref[rows, :] for rows in at], axis=0)
        shared = [jnp.where(sym == group, block[:, 8 * BASE :], nought) for group in groups]
        spilt = rows_dot(jnp.concatenate(shared, axis=1), spread).astype(BF16)
        for r, rows in enumerate(at):
            kept[rows, : 8 * BASE] = block[r * 16 : r * 16 + 16, : 8 * BASE]
            kept[rows, 8 * BASE :] = spilt[r * 16 : r * 16 + 16, :]
        return carry

    lax.fori_loop(0, 16, unpack, 0, unroll=8)

    even = core == 0
    chunk = 1024

    def multiply(n, carry):
        rows = pl.ds(pl.multiple_of(n * TILE, TILE), TILE)
        fetch(n).wait()
        m_sym = m_ref[rows, :]
        total = jnp.zeros((TILE, 256), F32)
        for at in range(0, depth, chunk):
            parts = []
            for start in range(at, at + chunk, LANES):
                lanes = slice(start, start + LANES)
                same = m_sym == jnp.broadcast_to(k_ref[0:1, lanes], m_sym.shape)
                parts.append(jnp.where(same, local[rows, lanes], nought))
            screened = jnp.concatenate(parts, axis=1)
            total += jnp.dot(screened, kept[at : at + chunk, :], preferred_element_type=F32)
        turned = jnp.transpose(total)
        for z in range(4):
            for half in range(2):
                at = half * 128 + z * 2 * BASE
                low, high = turned[at : at + BASE, :], turned[at + BASE : at + 2 * BASE, :]
                slots = slice(half * BASE, half * BASE + BASE)
                keep_ref[z, slots, rows] = jnp.where(even, low, high)
                send_ref[z, slots, rows] = jnp.where(even, high, low)
        return carry

    lax.fori_loop(0, tiles, multiply, 0)


def share_kernel(keep_ref, got_ref, own_ref, *out_refs):
    z = lax.axis_index("col") >> 1
    own_ref[...] = keep_ref[z] + got_ref[z]
    for step, out_ref in enumerate(out_refs):
        there = (z + step + 1) & 3
        total = keep_ref[there] + got_ref[there]
        largest = jnp.max(jnp.abs(total), axis=0, keepdims=True)
        power = jnp.minimum(jnp.floor(14.9 - jnp.log2(jnp.maximum(largest, 1e-37))), 120.0)
        scaled = total * jnp.exp2(power)
        scaled = jnp.where(iota(total.shape, 0) == CAP - 1, power, scaled)
        out_ref[...] = (scaled + jnp.where(scaled >= 0, 0.5, -0.5)).astype(I32).astype(jnp.int16)


def expand_kernel(own_ref, a_ref, b_ref, c_ref, m_ref, occ_ref, rank_ref, out_ref):
    lanes = pl.ds(pl.multiple_of(lax.axis_index("col") * LANES, LANES), LANES)
    total = own_ref[...]
    for ref in (a_ref, b_ref, c_ref):
        part = ref[...].astype(I32).astype(F32)
        total += part * jnp.exp2(-part[CAP - 1 : CAP, :])
    slot = iota((CAP, LANES), 0)
    pick = one_hot(slot == jnp.broadcast_to(rank_ref[0:1, lanes], (CAP, LANES)))
    wide = lax.dot_general(total.astype(BF16), pick, (((0,), (0,)), ((), ())), preferred_element_type=F32)
    same = m_ref[...].astype(F32) == jnp.broadcast_to(occ_ref[0:1, lanes].astype(F32), wide.shape)
    out_ref[...] = jnp.where(same, wide, 0.0).astype(BF16)


def plain_symbols_kernel(
    occ_ref, virt_ref, occ_orbs, k_orbs, m_orbs, own_orbs, occ_out, rank_out, k_out, m_out, own_out, most_out
):
    occ = pack_labels(occ_ref[0:1, :])
    virt = pack_labels(virt_ref[0:7, :])
    first = lax.broadcasted_iota(I32, (LANES, LANES), 0)
    second = lax.broadcasted_iota(I32, (LANES, LANES), 1)
    most = jnp.zeros((1, LANES), I32)
    for start in range(0, occ_orbs.shape[1], LANES):
        sym = pair_symbols(occ, occ_orbs, start)
        occ_out[:, start : start + LANES] = sym
        same = as_column(sym) == jnp.broadcast_to(sym[0:1, :].astype(F32), (LANES, LANES))
        earlier = jnp.where(same & (first < second), 1.0, 0.0)
        rank = jnp.sum(earlier, axis=0, keepdims=True).astype(I32)
        most = jnp.maximum(most, rank)
        rank_out[:, start : start + LANES] = jnp.broadcast_to(rank, (8, LANES))
    most_out[0, 0] = jnp.max(most)
    for start in range(0, k_orbs.shape[1], LANES):
        sym = pair_symbols(virt, k_orbs, start).astype(F32)
        k_out[:, start : start + LANES] = jnp.concatenate([sym, sym], axis=0).astype(BF16)
    for start in range(0, m_orbs.shape[1], LANES):
        m_out[start : start + LANES, :] = as_column(pair_symbols(virt, m_orbs, start)).astype(BF16)
    for start in range(0, own_orbs.shape[1], LANES):
        own_out[start : start + LANES, :] = as_column(pair_symbols(virt, own_orbs, start)).astype(I32)


def plain_compact_kernel(copies, pass_ref, rows_ref, own_ref, occ_ref, rank_ref, out_ref):
    n, pairs = rows_ref.shape
    cols = pairs // LANES
    i = lax.broadcasted_iota(I32, (n, n), 0)
    j = lax.broadcasted_iota(I32, (n, n), 1)
    wanted = ((i >> 1) & 7) * 32 + (i >> 4) * 2 + (i & 1)
    order = jnp.where(j == wanted, 1.0, 0.0).astype(BF16)
    rows = jnp.dot(order, rows_ref[...], preferred_element_type=F32)
    base = pass_ref[0] * CAP
    slot = lax.broadcasted_iota(I32, (CAP, LANES), 0) + base
    own = own_ref[...]
    for c in range(cols):
        lanes = slice(c * LANES, (c + 1) * LANES)
        keep = own == jnp.broadcast_to(occ_ref[0:1, lanes], (n, LANES))
        kept = jnp.where(keep, rows[:, lanes], 0.0).astype(BF16)
        pick = jnp.where(slot == jnp.broadcast_to(rank_ref[0:1, lanes], (CAP, LANES)), 1.0, 0.0).astype(BF16)
        part = lax.dot_general(kept, pick, (((1,), (1,)), ((), ())), preferred_element_type=F32).astype(BF16)
        for r in range(copies):
            out_ref[r, :, c * CAP : (c + 1) * CAP] = part


def plain_product_kernel(core_ref, amp_ref, int_ref, k_ref, m_ref, keep_ref, send_ref, kept):
    depth, width = amp_ref.shape
    block = depth // 16

    @pl.when(pl.program_id(0) == 0)
    def _():
        for r in range(16):
            for source in range(16):
                kept[r * block + source * 16 : r * block + source * 16 + 16, :] = amp_ref[
                    source * block + r * 16 : source * block + r * 16 + 16, :
                ]

    m_sym = m_ref[...]
    chunk = 1024
    total = jnp.zeros((m_ref.shape[0], width), F32)
    for at in range(0, depth, chunk):
        parts = []
        for lane in range(at, at + chunk, LANES):
            lanes = slice(lane, lane + LANES)
            same = m_sym == jnp.broadcast_to(k_ref[0:1, lanes], m_sym.shape)
            parts.append(jnp.where(same, int_ref[:, lanes], jnp.zeros((), BF16)))
        screened = jnp.concatenate(parts, axis=1)
        total += jnp.dot(screened, kept[at : at + chunk, :], preferred_element_type=F32)
    turned = jnp.transpose(total)
    even = core_ref[0] == 0
    for z in range(4):
        low = turned[z * 2 * CAP : z * 2 * CAP + CAP, :]
        high = turned[z * 2 * CAP + CAP : z * 2 * CAP + 2 * CAP, :]
        keep_ref[z] = jnp.where(even, low, high)
        send_ref[z] = jnp.where(even, high, low)


def plain_share_kernel(z_ref, keep_ref, got_ref, *out_refs):
    for step, out_ref in enumerate(out_refs):
        z = (z_ref[0] + step) % 4
        out_ref[...] = keep_ref[z] + got_ref[z]


def plain_expand_kernel(at_ref, a_ref, b_ref, c_ref, d_ref, m_ref, occ_ref, rank_ref, out_ref):
    lanes = pl.ds(pl.multiple_of(at_ref[0] * LANES, LANES), LANES)
    total = (a_ref[...] + b_ref[...] + c_ref[...] + d_ref[...]).astype(BF16)
    slot = lax.broadcasted_iota(I32, (CAP, LANES), 0) + at_ref[1] * CAP
    pick = jnp.where(slot == jnp.broadcast_to(rank_ref[0:1, lanes], (CAP, LANES)), 1.0, 0.0).astype(BF16)
    wide = lax.dot_general(total, pick, (((0,), (0,)), ((), ())), preferred_element_type=F32)
    same = m_ref[...].astype(F32) == jnp.broadcast_to(occ_ref[0:1, lanes].astype(F32), wide.shape)
    out_ref[...] = jnp.where(same, wide, 0.0).astype(BF16)


def params(mib=16):
    return pltpu.CompilerParams(vmem_limit_bytes=mib * 1024 * 1024)


def whole():
    return pl.BlockSpec(memory_space=pltpu.VMEM)


def scalars():
    return pl.BlockSpec(memory_space=pltpu.SMEM)


def plain(amp_store, store_map, integrals, occ_irrep, virt_irrep, occ_orbs, k_orbs, m_orbs):
    rows = lax.axis_size("row")
    cols = lax.axis_size("col")
    stored, pairs = amp_store.shape
    kblock = k_orbs.shape[1]
    m_dev = m_orbs.shape[1]
    my_row = lax.axis_index("row")
    my_col = lax.axis_index("col")
    shape = jax.ShapeDtypeStruct

    place = (store_map // kblock) * (rows * 2) + ((store_map % kblock) // stored) * 2 + store_map % 2
    order = (jnp.arange(stored, dtype=I32)[:, None] == place[None, :]).astype(BF16)
    ordered = jnp.dot(order, amp_store, preferred_element_type=F32).astype(BF16)
    column_rows = lax.all_to_all(ordered, "col", split_axis=0, concat_axis=0, tiled=True)

    own_orbs = lax.dynamic_slice_in_dim(k_orbs.reshape(2, rows, stored), my_row * 16, 16, axis=2).reshape(2, stored)
    occ_lab = jnp.pad(occ_irrep, (0, LANES - occ_irrep.shape[0])).reshape(1, LANES)
    virt_lab = jnp.pad(virt_irrep, (0, 8 * LANES - virt_irrep.shape[0])).reshape(8, LANES)
    occ_sym, rank, k_sym, m_sym, own_sym, most = pl.pallas_call(
        plain_symbols_kernel,
        out_shape=(
            shape((8, pairs), I32),
            shape((8, pairs), I32),
            shape((16, kblock), BF16),
            shape((m_dev, LANES), BF16),
            shape((stored, LANES), I32),
            shape((1, 1), I32),
        ),
        in_specs=[whole()] * 6,
        out_specs=(whole(),) * 5 + (scalars(),),
        compiler_params=params(),
        name="plain_symbols",
    )(occ_lab, virt_lab, occ_orbs, k_orbs, m_orbs, own_orbs)

    def one_pass(step):
        width = cols * CAP
        compact = pl.pallas_call(
            functools.partial(plain_compact_kernel, rows),
            out_shape=shape((rows, stored, width), BF16),
            in_specs=[scalars()] + [whole()] * 4,
            out_specs=whole(),
            compiler_params=params(),
            name="plain_compact",
        )(step.reshape(1), column_rows, own_sym, occ_sym, rank)
        gathered = lax.all_to_all(
            compact.reshape(rows * stored, width), "row", split_axis=0, concat_axis=0, tiled=True
        )
        keep, send = pl.pallas_call(
            plain_product_kernel,
            grid=(m_dev // TM,),
            out_shape=(shape((4, CAP, m_dev), F32),) * 2,
            in_specs=[
                scalars(),
                pl.BlockSpec((kblock, width), lambda i: (0, 0)),
                pl.BlockSpec((TM, kblock), lambda i: (i, 0)),
                pl.BlockSpec((16, kblock), lambda i: (0, 0)),
                pl.BlockSpec((TM, LANES), lambda i: (i, 0)),
            ],
            out_specs=(pl.BlockSpec((4, CAP, TM), lambda i: (0, 0, i)),) * 2,
            scratch_shapes=[pltpu.VMEM((kblock, width), BF16)],
            compiler_params=params(),
            name="plain_product",
        )((my_col % 2).reshape(1), gathered, integrals, k_sym, m_sym)
        got = lax.ppermute(send, "col", [(i, i ^ 1) for i in range(cols)])
        shares = pl.pallas_call(
            plain_share_kernel,
            out_shape=(shape((CAP, m_dev), F32),) * 4,
            in_specs=[scalars(), whole(), whole()],
            out_specs=(whole(),) * 4,
            compiler_params=params(),
            name="plain_share",
        )((my_col // 2).reshape(1), keep, got)
        sums = [shares[0]]
        for distance in range(1, 4):
            hops = [(i, (i + 2 * distance) % cols) for i in range(cols)]
            sums.append(lax.ppermute(shares[distance], "col", hops))
        return pl.pallas_call(
            plain_expand_kernel,
            out_shape=shape((m_dev, LANES), BF16),
            in_specs=[scalars()] + [whole()] * 7,
            out_specs=whole(),
            compiler_params=params(),
            name="plain_expand",
        )(jnp.stack([my_col, step]), *sums, m_sym, occ_sym, rank)

    passes = most[0, 0] // CAP + 1
    return lax.while_loop(
        lambda state: state[0] < passes,
        lambda state: (state[0] + 1, state[1] + one_pass(state[0])),
        (jnp.zeros((), I32), jnp.zeros((m_dev, LANES), BF16)),
    )[1]


def body(amp_store, store_map, integrals, occ_irrep, virt_irrep, occ_orbs, k_orbs, m_orbs):
    rows = lax.axis_size("row")
    cols = lax.axis_size("col")
    stored, pairs = amp_store.shape
    kblock = k_orbs.shape[1]
    m_dev = m_orbs.shape[1]
    shape = jax.ShapeDtypeStruct
    swap = [(i, i ^ 1) for i in range(cols)]
    hops = [[(i, (i + 2 * d) % cols) for i in range(cols)] for d in range(4)]

    def call(kernel, name, out_shape, operands, mib=16, **kw):
        return pl.pallas_call(
            kernel,
            out_shape=out_shape,
            in_specs=kw.pop("in_specs", [whole()] * len(operands)),
            out_specs=kw.pop("out_specs", jax.tree.map(lambda _: whole(), out_shape)),
            compiler_params=params(mib),
            name=name,
            **kw,
        )(*operands)

    ordered = call(order_kernel, "order", (shape((64, pairs), BF16),) * 4, (store_map.reshape(1, stored), amp_store))
    arrived = [ordered[0]] + [lax.ppermute(ordered[d], "col", hops[d]) for d in range(1, 4)]

    other_orbs = lax.ppermute(k_orbs, "col", swap)
    occ_lab = jnp.pad(occ_irrep, (0, LANES - occ_irrep.shape[0])).reshape(1, LANES)
    virt_lab = jnp.pad(virt_irrep, (0, 8 * LANES - virt_irrep.shape[0])).reshape(8, LANES)
    occ_sym, rank, place, spread, k_sym, k_col, m_sym, own_sym, other_sym, bad = call(
        symbols_kernel,
        "symbols",
        (
            shape((8, pairs), I32),
            shape((8, pairs), I32),
            shape((8, pairs), I32),
            shape((8 * BASE, 8 * ROOM), BF16),
            shape((16, kblock), BF16),
            shape((kblock, LANES), BF16),
            shape((m_dev, LANES), BF16),
            shape((LANES, LANES), F32),
            shape((LANES, LANES), F32),
            shape((1, 1), I32),
        ),
        (occ_lab, virt_lab, occ_orbs, k_orbs, m_orbs, other_orbs),
        out_specs=(whole(),) * 9 + (scalars(),),
        scratch_shapes=[pltpu.VMEM((kblock, LANES), BF16)],
    )

    mine, theirs = call(
        compact_kernel,
        "compact",
        (shape((PLACES, LANES), BF16),) * 2,
        (*arrived, own_sym, other_sym, occ_sym, place),
    )
    got = lax.ppermute(theirs, "col", swap)
    spreading = jnp.broadcast_to(jnp.concatenate([mine, got], axis=1)[None], (rows, PLACES, stored))
    gathered = lax.all_to_all(spreading, "row", split_axis=0, concat_axis=0, tiled=True)

    keep, send = call(
        product_kernel,
        "product",
        (shape((4, CAP, m_dev), F32),) * 2,
        (gathered, integrals, k_sym, k_col, m_sym, spread),
        30,
        in_specs=[whole(), pl.BlockSpec(memory_space=pl.ANY)] + [whole()] * 4,
        scratch_shapes=[
            pltpu.VMEM((kblock, 256), BF16),
            pltpu.VMEM((m_dev, kblock), BF16),
            pltpu.SemaphoreType.DMA((m_dev // TILE,)),
        ],
    )
    partner = lax.ppermute(send, "col", swap)
    shares = call(
        share_kernel,
        "share",
        (shape((CAP, m_dev), F32),) + (shape((CAP, m_dev), jnp.int16),) * 3,
        (keep, partner),
    )
    sums = [shares[0]] + [lax.ppermute(shares[d], "col", hops[d]) for d in range(1, 4)]
    result = call(expand_kernel, "expand", shape((m_dev, LANES), BF16), (*sums, m_sym, occ_sym, rank))

    return lax.cond(
        bad[0, 0] > 0,
        lambda: plain(amp_store, store_map, integrals, occ_irrep, virt_irrep, occ_orbs, k_orbs, m_orbs),
        lambda: result,
    )


def solution(mesh):
    in_specs = (
        P(("row", "col"), None),
        P(("row", "col")),
        P("row", "col"),
        P(),
        P(),
        P(),
        P(None, "col"),
        P(None, "row"),
    )
    out_specs = P("row", "col")
    return jax.shard_map(body, mesh=mesh, in_specs=in_specs, out_specs=out_specs, check_vma=False)
```

```python
import functools

import jax
import jax.numpy as jnp
from jax import lax
from jax.experimental import pallas as pl
from jax.experimental.pallas import tpu as pltpu
from jax.sharding import PartitionSpec as P

BF16 = jnp.bfloat16
F32 = jnp.float32
I32 = jnp.int32
LANES = 128
CAP = 32
BASE = 16
SPILL = 48
PLACES = 8 * BASE + SPILL
TM = 256


def pack_labels(labels):
    word = labels[0:1, :]
    for i in range(1, labels.shape[0]):
        word = word | (labels[i : i + 1, :] << (4 * i))
    return jnp.broadcast_to(word, (8, LANES))


def look_up(packed, orbitals):
    orbitals = jnp.broadcast_to(orbitals, (8, LANES))
    word = jnp.take_along_axis(packed, orbitals & (LANES - 1), axis=1)
    return (word >> ((orbitals >> 7) << 2)) & 7


def pair_symbols(packed, orbs_ref, start):
    lanes = pl.ds(start, LANES)
    return look_up(packed, orbs_ref[0:1, lanes]) ^ look_up(packed, orbs_ref[1:2, lanes])


def as_column(symbols):
    row = jnp.broadcast_to(symbols[0:1, :].astype(F32), (LANES, LANES))
    same = lax.broadcasted_iota(I32, (LANES, LANES), 0) == lax.broadcasted_iota(I32, (LANES, LANES), 1)
    diagonal = jnp.where(same, row, 0.0).astype(BF16)
    return jnp.dot(diagonal, jnp.ones((LANES, LANES), BF16), preferred_element_type=F32)


def one_hot(mask):
    return jnp.where(mask, 1.0, 0.0).astype(BF16)


def rows_dot(a, b):
    return lax.dot_general(a, b, (((1,), (1,)), ((), ())), preferred_element_type=F32)


def iota(shape, axis):
    return lax.broadcasted_iota(I32, shape, axis)


def order_kernel(map_ref, amp_ref, *out_refs):
    z, core = lax.axis_index("col") >> 1, lax.axis_index("col") & 1
    k = map_ref[...]
    col, row, within = k >> 12, (k >> 8) & 15, k & 1
    place = ((((col >> 1) - z) & 3) * 2 + ((col & 1) ^ core)) * 32 + row * 2 + within
    n = amp_ref.shape[0]
    order = one_hot(iota((n, n), 0) == jnp.broadcast_to(place, (n, n)))
    rows = jnp.dot(order, amp_ref[...], preferred_element_type=F32).astype(BF16)
    for d, out_ref in enumerate(out_refs):
        out_ref[...] = rows[d * 64 : d * 64 + 64, :]


def symbols_kernel(
    labels_ref, occ_orbs, k_orbs, m_orbs, other_orbs, int_ref,
    occ_out, rank_out, place_out, from_out, k_out, m_out, own_out, other_out, early, bad_out, own_col, other_col, sem,
):
    core = lax.axis_index("col") & 1
    occ = pack_labels(labels_ref[7:8, :])
    virt = pack_labels(labels_ref[0:7, :])
    first = iota((LANES, LANES), 0)
    second = iota((LANES, LANES), 1)
    group = iota((8, LANES), 0)
    used = jnp.zeros((8, 1), I32)
    bad = jnp.zeros((1, LANES), I32)
    lane = iota((8, LANES), 1)
    table = jnp.full((8, LANES), LANES - 1, I32)
    for c in range(occ_orbs.shape[1] // LANES):
        lanes = slice(c * LANES, (c + 1) * LANES)
        sym = pair_symbols(occ, occ_orbs, c * LANES)
        occ_out[:, lanes] = sym
        same = as_column(sym) == jnp.broadcast_to(sym[0:1, :].astype(F32), (LANES, LANES))
        rank = jnp.sum(jnp.where(same & (first < second), 1.0, 0.0), axis=0, keepdims=True).astype(I32)
        rank_out[:, lanes] = jnp.broadcast_to(rank, (8, LANES))
        mine = sym == group
        extra = jnp.sum(jnp.where(mine, used, 0), axis=0, keepdims=True) + rank - BASE
        over = jnp.maximum(jnp.sum(jnp.where(mine, 1, 0), axis=1, keepdims=True) - BASE, 0)
        at = lane - c * BASE
        table = jnp.where((at >= 0) & (at < jnp.minimum(over, BASE)) & (used + at < SPILL), used + at, table)
        used = used + over
        spilt = rank >= BASE
        bad = jnp.maximum(bad, jnp.where(spilt & ((extra >= SPILL) | (rank >= CAP - 1)), 1, 0))
        place = jnp.where(spilt, jnp.where(extra < SPILL, 8 * BASE + extra, -1), c * BASE + rank)
        place_out[:, lanes] = jnp.broadcast_to(place, (8, LANES))
    bad_out[0, 0] = jnp.max(bad)
    table = jnp.concatenate([table.astype(F32), jnp.zeros((LANES - 8, LANES), F32)], axis=0).astype(BF16)

    step = early.shape[0] * LANES // k_orbs.shape[1]

    def contracted(n, carry):
        some = pl.ds(pl.multiple_of(n * step, step), step)
        pltpu.make_async_copy(int_ref.at[some], early.at[some], sem).start()
        start = pl.multiple_of(n * LANES, LANES)
        rows = pl.ds(start, LANES)
        sym = pair_symbols(virt, k_orbs, start)
        wide = sym.astype(F32)
        k_out[:, rows] = jnp.concatenate([wide, wide], axis=0).astype(BF16)
        column = as_column(sym)
        own_col[rows, :] = column.astype(BF16)
        group = one_hot(column == second.astype(F32))
        from_out[rows, :] = jnp.dot(group, table, preferred_element_type=F32).astype(I32)
        return carry

    lax.fori_loop(0, k_orbs.shape[1] // LANES, contracted, 0, unroll=8)

    def output(n, carry):
        start = pl.multiple_of(n * LANES, LANES)
        m_out[pl.ds(start, LANES), :] = as_column(pair_symbols(virt, m_orbs, start)).astype(BF16)
        return carry

    lax.fori_loop(0, m_orbs.shape[1] // LANES, output, 0, unroll=8)

    i, j = iota((LANES, 2 * LANES), 0), iota((LANES, 2 * LANES), 1)
    pick = one_hot(j == (i >> 1) * 4 + core * 2 + (i & 1))
    mine = lax.axis_index("row") * 16
    tile = pl.multiple_of(mine & LANES, LANES)
    for r in range(16):
        other_col[r * LANES : (r + 1) * LANES, :] = as_column(
            pair_symbols(virt, other_orbs, r * 256 + tile)
        ).astype(BF16)
    inside = pl.multiple_of(mine & (LANES - 1), 16)
    for ref, out, far, at in ((own_col, own_out, 256, pl.multiple_of(mine, 16)), (other_col, other_out, LANES, inside)):
        column = jnp.concatenate([ref[pl.ds(r * far + at, 16), :] for r in range(16)], axis=0)
        out[...] = jnp.dot(pick, column, preferred_element_type=F32)
    pltpu.make_async_copy(int_ref.at[pl.ds(0, early.shape[0])], early, sem).wait()


def compact_kernel(a_ref, b_ref, c_ref, d_ref, own_ref, other_ref, occ_ref, place_ref, mine_out, theirs_out):
    z = lax.axis_index("col") >> 1
    rows = jnp.concatenate([a_ref[...], b_ref[...], c_ref[...], d_ref[...]], axis=0)
    pairs = rows.shape[1]
    squeeze = one_hot(iota((PLACES, pairs), 0) == jnp.broadcast_to(place_ref[0:1, :], (PLACES, pairs)))
    occ = jnp.broadcast_to(occ_ref[0:1, :].astype(F32), (LANES, pairs))
    i, j = iota((LANES, 2 * LANES), 0), iota((LANES, 2 * LANES), 1)
    row, source, within = i >> 3, (i >> 1) & 3, i & 1
    for side, sym_ref, out in ((0, own_ref, mine_out), (1, other_ref, theirs_out)):
        order = one_hot(j == (((z - source) & 3) * 2 + side) * 32 + row * 2 + within)
        turned = jnp.dot(order, rows, preferred_element_type=F32)
        sym = jnp.concatenate([sym_ref[...]] * (pairs // LANES), axis=1)
        kept = jnp.where(sym == occ, turned, 0.0).astype(BF16)
        out[...] = rows_dot(squeeze, kept).astype(BF16)


def multiply(rows_ref, kept_ref, k_ref, m_sym, keep_ref, send_ref):
    even = (lax.axis_index("col") & 1) == 0
    depth, chunk = k_ref.shape[1], 1024
    total = jnp.zeros((m_sym.shape[0], 256), F32)
    for at in range(0, depth, chunk):
        parts = []
        for start in range(at, at + chunk, LANES):
            lanes = slice(start, start + LANES)
            same = m_sym == jnp.broadcast_to(k_ref[0:1, lanes], m_sym.shape)
            parts.append(jnp.where(same, rows_ref[:, lanes], jnp.zeros((), BF16)))
        screened = jnp.concatenate(parts, axis=1)
        total += jnp.dot(screened, kept_ref[at : at + chunk, :], preferred_element_type=F32)
    turned = jnp.transpose(total)
    for z in range(4):
        for half in range(2):
            at = half * 128 + z * 2 * BASE
            low, high = turned[at : at + BASE, :], turned[at + BASE : at + 2 * BASE, :]
            slots = slice(half * BASE, half * BASE + BASE)
            keep_ref[z, slots, :] = jnp.where(even, low, high)
            send_ref[z, slots, :] = jnp.where(even, high, low)


def first_kernel(amp_ref, early, int_ref, k_ref, from_ref, m_ref, keep_ref, send_ref, kept, later, sem):
    core = lax.axis_index("col") & 1
    half = early.shape[0]
    fetch = pltpu.make_async_copy(int_ref.at[pl.ds(half, half)], later, sem)
    fetch.start()

    i, j = iota((256, 256), 0), iota((256, 256), 1)
    order = one_hot(j == (((i >> 1) & 1) ^ core) * 128 + (i >> 4) * 8 + ((i >> 2) & 3) * 2 + (i & 1))
    gap = jnp.zeros((256 - PLACES, 256), BF16)

    def unpack(source, carry):
        block = rows_dot(order, jnp.concatenate([amp_ref[source], gap], axis=0))
        at = [pl.ds(pl.multiple_of(r * 256 + source * 16, 16), 16) for r in range(16)]
        main = block[:, : 8 * BASE].astype(BF16)
        for r, rows in enumerate(at):
            shared = block[r * 16 : r * 16 + 16, 8 * BASE :]
            index = from_ref[rows, :]
            spilt = [jnp.take_along_axis(shared[h : h + 8], index[h : h + 8], axis=1) for h in (0, 8)]
            kept[rows, : 8 * BASE] = main[r * 16 : r * 16 + 16, :]
            kept[rows, 8 * BASE :] = jnp.concatenate(spilt, axis=0).astype(BF16)
        return carry

    lax.fori_loop(0, 16, unpack, 0, unroll=8)
    multiply(early, kept, k_ref, m_ref[:half, :], keep_ref, send_ref)
    fetch.wait()


def second_kernel(int_ref, kept_ref, k_ref, m_ref, keep_ref, send_ref):
    half = int_ref.shape[0]
    multiply(int_ref, kept_ref, k_ref, m_ref[half:, :], keep_ref, send_ref)


def share_kernel(keep_ref, got_ref, own_ref, *out_refs):
    z = lax.axis_index("col") >> 1
    own_ref[...] = keep_ref[z] + got_ref[z]
    for step, out_ref in enumerate(out_refs):
        there = (z + step + 1) & 3
        total = keep_ref[there] + got_ref[there]
        largest = jnp.max(jnp.abs(total), axis=0, keepdims=True)
        power = jnp.minimum(jnp.floor(14.9 - jnp.log2(jnp.maximum(largest, 1e-37))), 120.0)
        scaled = total * jnp.exp2(power)
        scaled = jnp.where(iota(total.shape, 0) == CAP - 1, power, scaled)
        out_ref[...] = (scaled + jnp.where(scaled >= 0, 0.5, -0.5)).astype(I32).astype(jnp.int16)


def expand_kernel(*refs):
    m_ref, occ_ref, rank_ref, out_ref = refs[-4:]
    lanes = pl.ds(pl.multiple_of(lax.axis_index("col") * LANES, LANES), LANES)
    slot = iota((CAP, LANES), 0)
    pick = one_hot(slot == jnp.broadcast_to(rank_ref[0:1, lanes], (CAP, LANES)))
    half = refs[0].shape[1]
    for part in range(2):
        total = refs[part * 4][...]
        for ref in refs[part * 4 + 1 : part * 4 + 4]:
            got = ref[...].astype(I32).astype(F32)
            total += got * jnp.exp2(-got[CAP - 1 : CAP, :])
        rows = slice(part * half, part * half + half)
        wide = lax.dot_general(total.astype(BF16), pick, (((0,), (0,)), ((), ())), preferred_element_type=F32)
        same = m_ref[rows, :].astype(F32) == jnp.broadcast_to(occ_ref[0:1, lanes].astype(F32), wide.shape)
        out_ref[rows, :] = jnp.where(same, wide, 0.0).astype(BF16)


def plain_symbols_kernel(
    occ_ref, virt_ref, occ_orbs, k_orbs, m_orbs, own_orbs, occ_out, rank_out, k_out, m_out, own_out, most_out
):
    occ = pack_labels(occ_ref[0:1, :])
    virt = pack_labels(virt_ref[0:7, :])
    first = lax.broadcasted_iota(I32, (LANES, LANES), 0)
    second = lax.broadcasted_iota(I32, (LANES, LANES), 1)
    most = jnp.zeros((1, LANES), I32)
    for start in range(0, occ_orbs.shape[1], LANES):
        sym = pair_symbols(occ, occ_orbs, start)
        occ_out[:, start : start + LANES] = sym
        same = as_column(sym) == jnp.broadcast_to(sym[0:1, :].astype(F32), (LANES, LANES))
        earlier = jnp.where(same & (first < second), 1.0, 0.0)
        rank = jnp.sum(earlier, axis=0, keepdims=True).astype(I32)
        most = jnp.maximum(most, rank)
        rank_out[:, start : start + LANES] = jnp.broadcast_to(rank, (8, LANES))
    most_out[0, 0] = jnp.max(most)
    for start in range(0, k_orbs.shape[1], LANES):
        sym = pair_symbols(virt, k_orbs, start).astype(F32)
        k_out[:, start : start + LANES] = jnp.concatenate([sym, sym], axis=0).astype(BF16)
    for start in range(0, m_orbs.shape[1], LANES):
        m_out[start : start + LANES, :] = as_column(pair_symbols(virt, m_orbs, start)).astype(BF16)
    for start in range(0, own_orbs.shape[1], LANES):
        own_out[start : start + LANES, :] = as_column(pair_symbols(virt, own_orbs, start)).astype(I32)


def plain_compact_kernel(copies, pass_ref, rows_ref, own_ref, occ_ref, rank_ref, out_ref):
    n, pairs = rows_ref.shape
    cols = pairs // LANES
    i = lax.broadcasted_iota(I32, (n, n), 0)
    j = lax.broadcasted_iota(I32, (n, n), 1)
    wanted = ((i >> 1) & 7) * 32 + (i >> 4) * 2 + (i & 1)
    order = jnp.where(j == wanted, 1.0, 0.0).astype(BF16)
    rows = jnp.dot(order, rows_ref[...], preferred_element_type=F32)
    base = pass_ref[0] * CAP
    slot = lax.broadcasted_iota(I32, (CAP, LANES), 0) + base
    own = own_ref[...]
    for c in range(cols):
        lanes = slice(c * LANES, (c + 1) * LANES)
        keep = own == jnp.broadcast_to(occ_ref[0:1, lanes], (n, LANES))
        kept = jnp.where(keep, rows[:, lanes], 0.0).astype(BF16)
        pick = jnp.where(slot == jnp.broadcast_to(rank_ref[0:1, lanes], (CAP, LANES)), 1.0, 0.0).astype(BF16)
        part = lax.dot_general(kept, pick, (((1,), (1,)), ((), ())), preferred_element_type=F32).astype(BF16)
        for r in range(copies):
            out_ref[r, :, c * CAP : (c + 1) * CAP] = part


def plain_product_kernel(core_ref, amp_ref, int_ref, k_ref, m_ref, keep_ref, send_ref, kept):
    depth, width = amp_ref.shape
    block = depth // 16

    @pl.when(pl.program_id(0) == 0)
    def _():
        for r in range(16):
            for source in range(16):
                kept[r * block + source * 16 : r * block + source * 16 + 16, :] = amp_ref[
                    source * block + r * 16 : source * block + r * 16 + 16, :
                ]

    m_sym = m_ref[...]
    chunk = 1024
    total = jnp.zeros((m_ref.shape[0], width), F32)
    for at in range(0, depth, chunk):
        parts = []
        for lane in range(at, at + chunk, LANES):
            lanes = slice(lane, lane + LANES)
            same = m_sym == jnp.broadcast_to(k_ref[0:1, lanes], m_sym.shape)
            parts.append(jnp.where(same, int_ref[:, lanes], jnp.zeros((), BF16)))
        screened = jnp.concatenate(parts, axis=1)
        total += jnp.dot(screened, kept[at : at + chunk, :], preferred_element_type=F32)
    turned = jnp.transpose(total)
    even = core_ref[0] == 0
    for z in range(4):
        low = turned[z * 2 * CAP : z * 2 * CAP + CAP, :]
        high = turned[z * 2 * CAP + CAP : z * 2 * CAP + 2 * CAP, :]
        keep_ref[z] = jnp.where(even, low, high)
        send_ref[z] = jnp.where(even, high, low)


def plain_share_kernel(z_ref, keep_ref, got_ref, *out_refs):
    for step, out_ref in enumerate(out_refs):
        z = (z_ref[0] + step) % 4
        out_ref[...] = keep_ref[z] + got_ref[z]


def plain_expand_kernel(at_ref, a_ref, b_ref, c_ref, d_ref, m_ref, occ_ref, rank_ref, out_ref):
    lanes = pl.ds(pl.multiple_of(at_ref[0] * LANES, LANES), LANES)
    total = (a_ref[...] + b_ref[...] + c_ref[...] + d_ref[...]).astype(BF16)
    slot = lax.broadcasted_iota(I32, (CAP, LANES), 0) + at_ref[1] * CAP
    pick = jnp.where(slot == jnp.broadcast_to(rank_ref[0:1, lanes], (CAP, LANES)), 1.0, 0.0).astype(BF16)
    wide = lax.dot_general(total, pick, (((0,), (0,)), ((), ())), preferred_element_type=F32)
    same = m_ref[...].astype(F32) == jnp.broadcast_to(occ_ref[0:1, lanes].astype(F32), wide.shape)
    out_ref[...] = jnp.where(same, wide, 0.0).astype(BF16)


def params(mib=16):
    return pltpu.CompilerParams(vmem_limit_bytes=mib * 1024 * 1024)


def whole():
    return pl.BlockSpec(memory_space=pltpu.VMEM)


def scalars():
    return pl.BlockSpec(memory_space=pltpu.SMEM)


def plain(amp_store, store_map, integrals, occ_irrep, virt_irrep, occ_orbs, k_orbs, m_orbs):
    rows = lax.axis_size("row")
    cols = lax.axis_size("col")
    stored, pairs = amp_store.shape
    kblock = k_orbs.shape[1]
    m_dev = m_orbs.shape[1]
    my_row = lax.axis_index("row")
    my_col = lax.axis_index("col")
    shape = jax.ShapeDtypeStruct

    place = (store_map // kblock) * (rows * 2) + ((store_map % kblock) // stored) * 2 + store_map % 2
    order = (jnp.arange(stored, dtype=I32)[:, None] == place[None, :]).astype(BF16)
    ordered = jnp.dot(order, amp_store, preferred_element_type=F32).astype(BF16)
    column_rows = lax.all_to_all(ordered, "col", split_axis=0, concat_axis=0, tiled=True)

    own_orbs = lax.dynamic_slice_in_dim(k_orbs.reshape(2, rows, stored), my_row * 16, 16, axis=2).reshape(2, stored)
    occ_lab = jnp.pad(occ_irrep, (0, LANES - occ_irrep.shape[0])).reshape(1, LANES)
    virt_lab = jnp.pad(virt_irrep, (0, 8 * LANES - virt_irrep.shape[0])).reshape(8, LANES)
    occ_sym, rank, k_sym, m_sym, own_sym, most = pl.pallas_call(
        plain_symbols_kernel,
        out_shape=(
            shape((8, pairs), I32),
            shape((8, pairs), I32),
            shape((16, kblock), BF16),
            shape((m_dev, LANES), BF16),
            shape((stored, LANES), I32),
            shape((1, 1), I32),
        ),
        in_specs=[whole()] * 6,
        out_specs=(whole(),) * 5 + (scalars(),),
        compiler_params=params(),
        name="plain_symbols",
    )(occ_lab, virt_lab, occ_orbs, k_orbs, m_orbs, own_orbs)

    def one_pass(step):
        width = cols * CAP
        compact = pl.pallas_call(
            functools.partial(plain_compact_kernel, rows),
            out_shape=shape((rows, stored, width), BF16),
            in_specs=[scalars()] + [whole()] * 4,
            out_specs=whole(),
            compiler_params=params(),
            name="plain_compact",
        )(step.reshape(1), column_rows, own_sym, occ_sym, rank)
        gathered = lax.all_to_all(
            compact.reshape(rows * stored, width), "row", split_axis=0, concat_axis=0, tiled=True
        )
        keep, send = pl.pallas_call(
            plain_product_kernel,
            grid=(m_dev // TM,),
            out_shape=(shape((4, CAP, m_dev), F32),) * 2,
            in_specs=[
                scalars(),
                pl.BlockSpec((kblock, width), lambda i: (0, 0)),
                pl.BlockSpec((TM, kblock), lambda i: (i, 0)),
                pl.BlockSpec((16, kblock), lambda i: (0, 0)),
                pl.BlockSpec((TM, LANES), lambda i: (i, 0)),
            ],
            out_specs=(pl.BlockSpec((4, CAP, TM), lambda i: (0, 0, i)),) * 2,
            scratch_shapes=[pltpu.VMEM((kblock, width), BF16)],
            compiler_params=params(),
            name="plain_product",
        )((my_col % 2).reshape(1), gathered, integrals, k_sym, m_sym)
        got = lax.ppermute(send, "col", [(i, i ^ 1) for i in range(cols)])
        shares = pl.pallas_call(
            plain_share_kernel,
            out_shape=(shape((CAP, m_dev), F32),) * 4,
            in_specs=[scalars(), whole(), whole()],
            out_specs=(whole(),) * 4,
            compiler_params=params(),
            name="plain_share",
        )((my_col // 2).reshape(1), keep, got)
        sums = [shares[0]]
        for distance in range(1, 4):
            hops = [(i, (i + 2 * distance) % cols) for i in range(cols)]
            sums.append(lax.ppermute(shares[distance], "col", hops))
        return pl.pallas_call(
            plain_expand_kernel,
            out_shape=shape((m_dev, LANES), BF16),
            in_specs=[scalars()] + [whole()] * 7,
            out_specs=whole(),
            compiler_params=params(),
            name="plain_expand",
        )(jnp.stack([my_col, step]), *sums, m_sym, occ_sym, rank)

    passes = most[0, 0] // CAP + 1
    return lax.while_loop(
        lambda state: state[0] < passes,
        lambda state: (state[0] + 1, state[1] + one_pass(state[0])),
        (jnp.zeros((), I32), jnp.zeros((m_dev, LANES), BF16)),
    )[1]


def body(amp_store, store_map, integrals, occ_irrep, virt_irrep, occ_orbs, k_orbs, m_orbs):
    rows = lax.axis_size("row")
    cols = lax.axis_size("col")
    stored, pairs = amp_store.shape
    kblock = k_orbs.shape[1]
    m_dev = m_orbs.shape[1]
    shape = jax.ShapeDtypeStruct
    swap = [(i, i ^ 1) for i in range(cols)]
    hops = [[(i, (i + 2 * d) % cols) for i in range(cols)] for d in range(4)]

    def call(kernel, name, out_shape, operands, mib=16, **kw):
        return pl.pallas_call(
            kernel,
            out_shape=out_shape,
            in_specs=kw.pop("in_specs", [whole()] * len(operands)),
            out_specs=kw.pop("out_specs", jax.tree.map(lambda _: whole(), out_shape)),
            compiler_params=params(mib),
            name=name,
            **kw,
        )(*operands)

    ordered = call(order_kernel, "order", (shape((64, pairs), BF16),) * 4, (store_map.reshape(1, stored), amp_store))
    arrived = [ordered[0]] + [lax.ppermute(ordered[d], "col", hops[d]) for d in range(1, 4)]

    other_orbs = lax.ppermute(k_orbs, "col", swap)
    labels = jnp.concatenate(
        [jnp.pad(virt_irrep, (0, 7 * LANES - virt_irrep.shape[0])), jnp.pad(occ_irrep, (0, LANES - occ_irrep.shape[0]))]
    ).reshape(8, LANES)
    half = m_dev // 2
    occ_sym, rank, place, origin, k_sym, m_sym, own_sym, other_sym, early, bad = call(
        symbols_kernel,
        "symbols",
        (
            shape((8, pairs), I32),
            shape((8, pairs), I32),
            shape((8, pairs), I32),
            shape((kblock, LANES), I32),
            shape((16, kblock), BF16),
            shape((m_dev, LANES), BF16),
            shape((LANES, LANES), F32),
            shape((LANES, LANES), F32),
            shape((half, kblock), BF16),
            shape((1, 1), I32),
        ),
        (labels, occ_orbs, k_orbs, m_orbs, other_orbs, integrals),
        in_specs=[whole()] * 5 + [pl.BlockSpec(memory_space=pl.ANY)],
        out_specs=(whole(),) * 9 + (scalars(),),
        scratch_shapes=[
            pltpu.VMEM((kblock, LANES), BF16),
            pltpu.VMEM((kblock // 2, LANES), BF16),
            pltpu.SemaphoreType.DMA,
        ],
    )

    mine, theirs = call(
        compact_kernel,
        "compact",
        (shape((PLACES, LANES), BF16),) * 2,
        (*arrived, own_sym, other_sym, occ_sym, place),
    )
    got = lax.ppermute(theirs, "col", swap)
    spreading = jnp.broadcast_to(jnp.concatenate([mine, got], axis=1)[None], (rows, PLACES, stored))
    gathered = lax.all_to_all(spreading, "row", split_axis=0, concat_axis=0, tiled=True)

    pieces = (shape((4, CAP, half), F32),) * 2
    *first, kept, later = call(
        first_kernel,
        "first",
        pieces + (shape((kblock, 256), BF16), shape((half, kblock), BF16)),
        (gathered, early, integrals, k_sym, origin, m_sym),
        20,
        in_specs=[whole()] * 2 + [pl.BlockSpec(memory_space=pl.ANY)] + [whole()] * 3,
        scratch_shapes=[pltpu.SemaphoreType.DMA],
    )
    second = call(
        second_kernel,
        "second",
        pieces,
        (later, kept, k_sym, m_sym),
        12,
        cost_estimate=pl.CostEstimate(flops=half * kblock * 512, bytes_accessed=half * kblock * 2, transcendentals=0),
    )
    sums = []
    for keep, send in (first, second):
        partner = lax.ppermute(send, "col", swap)
        shares = call(
            share_kernel,
            "share",
            (shape((CAP, half), F32),) + (shape((CAP, half), jnp.int16),) * 3,
            (keep, partner),
        )
        sums += [shares[0]] + [lax.ppermute(shares[d], "col", hops[d]) for d in range(1, 4)]
    result = call(expand_kernel, "expand", shape((m_dev, LANES), BF16), (*sums, m_sym, occ_sym, rank))

    return lax.cond(
        bad[0, 0] > 0,
        lambda: plain(amp_store, store_map, integrals, occ_irrep, virt_irrep, occ_orbs, k_orbs, m_orbs),
        lambda: result,
    )


def solution(mesh):
    in_specs = (
        P(("row", "col"), None),
        P(("row", "col")),
        P("row", "col"),
        P(),
        P(),
        P(),
        P(None, "col"),
        P(None, "row"),
    )
    out_specs = P("row", "col")
    return jax.shard_map(body, mesh=mesh, in_specs=in_specs, out_specs=out_specs, check_vma=False)
```

```python
import functools

import jax
import jax.numpy as jnp
from jax import lax
from jax.experimental import pallas as pl
from jax.experimental.pallas import tpu as pltpu
from jax.sharding import PartitionSpec as P

BF16 = jnp.bfloat16
F32 = jnp.float32
I32 = jnp.int32
LANES = 128
CAP = 32
BASE = 16
SPILL = 48
PLACES = 8 * BASE + SPILL
TM = 256


def pack_labels(labels):
    word = labels[0:1, :]
    for i in range(1, labels.shape[0]):
        word = word | (labels[i : i + 1, :] << (4 * i))
    return jnp.broadcast_to(word, (8, LANES))


def look_up(packed, orbitals):
    orbitals = jnp.broadcast_to(orbitals, (8, LANES))
    word = jnp.take_along_axis(packed, orbitals & (LANES - 1), axis=1)
    return (word >> ((orbitals >> 7) << 2)) & 7


def pair_symbols(packed, orbs_ref, start):
    lanes = pl.ds(start, LANES)
    return look_up(packed, orbs_ref[0:1, lanes]) ^ look_up(packed, orbs_ref[1:2, lanes])


def as_column(symbols):
    row = jnp.broadcast_to(symbols[0:1, :].astype(F32), (LANES, LANES))
    same = lax.broadcasted_iota(I32, (LANES, LANES), 0) == lax.broadcasted_iota(I32, (LANES, LANES), 1)
    diagonal = jnp.where(same, row, 0.0).astype(BF16)
    return jnp.dot(diagonal, jnp.ones((LANES, LANES), BF16), preferred_element_type=F32)


def one_hot(mask):
    return jnp.where(mask, 1.0, 0.0).astype(BF16)


def rows_dot(a, b):
    return lax.dot_general(a, b, (((1,), (1,)), ((), ())), preferred_element_type=F32)


def iota(shape, axis):
    return lax.broadcasted_iota(I32, shape, axis)


def order_kernel(map_ref, amp_ref, *out_refs):
    z, core = lax.axis_index("col") >> 1, lax.axis_index("col") & 1
    k = map_ref[...]
    col, row, within = k >> 12, (k >> 8) & 15, k & 1
    place = ((((col >> 1) - z) & 3) * 2 + ((col & 1) ^ core)) * 32 + row * 2 + within
    n = amp_ref.shape[0]
    order = one_hot(iota((n, n), 0) == jnp.broadcast_to(place, (n, n)))
    rows = jnp.dot(order, amp_ref[...], preferred_element_type=F32).astype(BF16)
    for d, out_ref in enumerate(out_refs):
        out_ref[...] = rows[d * 64 : d * 64 + 64, :]


def symbols_kernel(
    labels_ref, occ_orbs, k_orbs, other_orbs, int_ref,
    occ_out, rank_out, place_out, from_out, k_out, own_out, other_out, early, bad_out, own_col, other_col, sem,
):
    core = lax.axis_index("col") & 1
    occ = pack_labels(labels_ref[7:8, :])
    virt = pack_labels(labels_ref[0:7, :])
    first = iota((LANES, LANES), 0)
    second = iota((LANES, LANES), 1)
    group = iota((8, LANES), 0)
    used = jnp.zeros((8, 1), I32)
    bad = jnp.zeros((1, LANES), I32)
    lane = iota((8, LANES), 1)
    table = jnp.full((8, LANES), LANES - 1, I32)
    for c in range(occ_orbs.shape[1] // LANES):
        lanes = slice(c * LANES, (c + 1) * LANES)
        sym = pair_symbols(occ, occ_orbs, c * LANES)
        occ_out[:, lanes] = sym
        same = as_column(sym) == jnp.broadcast_to(sym[0:1, :].astype(F32), (LANES, LANES))
        rank = jnp.sum(jnp.where(same & (first < second), 1.0, 0.0), axis=0, keepdims=True).astype(I32)
        rank_out[:, lanes] = jnp.broadcast_to(rank, (8, LANES))
        mine = sym == group
        extra = jnp.sum(jnp.where(mine, used, 0), axis=0, keepdims=True) + rank - BASE
        over = jnp.maximum(jnp.sum(jnp.where(mine, 1, 0), axis=1, keepdims=True) - BASE, 0)
        at = lane - c * BASE
        table = jnp.where((at >= 0) & (at < jnp.minimum(over, BASE)) & (used + at < SPILL), used + at, table)
        used = used + over
        spilt = rank >= BASE
        bad = jnp.maximum(bad, jnp.where(spilt & ((extra >= SPILL) | (rank >= CAP - 1)), 1, 0))
        place = jnp.where(spilt, jnp.where(extra < SPILL, 8 * BASE + extra, -1), c * BASE + rank)
        place_out[:, lanes] = jnp.broadcast_to(place, (8, LANES))
    bad_out[0, 0] = jnp.max(bad)
    table = jnp.concatenate([table.astype(F32), jnp.zeros((LANES - 8, LANES), F32)], axis=0).astype(BF16)

    step = early.shape[0] * LANES // k_orbs.shape[1]

    def contracted(n, carry):
        some = pl.ds(pl.multiple_of(n * step, step), step)
        pltpu.make_async_copy(int_ref.at[some], early.at[some], sem).start()
        start = pl.multiple_of(n * LANES, LANES)
        rows = pl.ds(start, LANES)
        sym = pair_symbols(virt, k_orbs, start)
        wide = sym.astype(F32)
        k_out[:, rows] = jnp.concatenate([wide, wide], axis=0).astype(BF16)
        column = as_column(sym)
        own_col[rows, :] = column.astype(BF16)
        group = one_hot(column == second.astype(F32))
        from_out[rows, :] = jnp.dot(group, table, preferred_element_type=F32).astype(I32)
        return carry

    lax.fori_loop(0, k_orbs.shape[1] // LANES, contracted, 0, unroll=8)

    i, j = iota((LANES, 2 * LANES), 0), iota((LANES, 2 * LANES), 1)
    pick = one_hot(j == (i >> 1) * 4 + core * 2 + (i & 1))
    mine = lax.axis_index("row") * 16
    tile = pl.multiple_of(mine & LANES, LANES)
    for r in range(16):
        other_col[r * LANES : (r + 1) * LANES, :] = as_column(
            pair_symbols(virt, other_orbs, r * 256 + tile)
        ).astype(BF16)
    inside = pl.multiple_of(mine & (LANES - 1), 16)
    for ref, out, far, at in ((own_col, own_out, 256, pl.multiple_of(mine, 16)), (other_col, other_out, LANES, inside)):
        column = jnp.concatenate([ref[pl.ds(r * far + at, 16), :] for r in range(16)], axis=0)
        out[...] = jnp.dot(pick, column, preferred_element_type=F32)
    pltpu.make_async_copy(int_ref.at[pl.ds(0, early.shape[0])], early, sem).wait()


def outputs_kernel(labels_ref, m_orbs, m_out):
    virt = pack_labels(labels_ref[0:7, :])

    def output(n, carry):
        start = pl.multiple_of(n * LANES, LANES)
        m_out[pl.ds(start, LANES), :] = as_column(pair_symbols(virt, m_orbs, start)).astype(BF16)
        return carry

    lax.fori_loop(0, m_orbs.shape[1] // LANES, output, 0, unroll=8)


def compact_kernel(a_ref, b_ref, c_ref, d_ref, own_ref, other_ref, occ_ref, place_ref, mine_out, theirs_out):
    z = lax.axis_index("col") >> 1
    rows = jnp.concatenate([a_ref[...], b_ref[...], c_ref[...], d_ref[...]], axis=0)
    pairs = rows.shape[1]
    squeeze = one_hot(iota((PLACES, pairs), 0) == jnp.broadcast_to(place_ref[0:1, :], (PLACES, pairs)))
    occ = jnp.broadcast_to(occ_ref[0:1, :].astype(F32), (LANES, pairs))
    i, j = iota((LANES, 2 * LANES), 0), iota((LANES, 2 * LANES), 1)
    row, source, within = i >> 3, (i >> 1) & 3, i & 1
    for side, sym_ref, out in ((0, own_ref, mine_out), (1, other_ref, theirs_out)):
        order = one_hot(j == (((z - source) & 3) * 2 + side) * 32 + row * 2 + within)
        turned = jnp.dot(order, rows, preferred_element_type=F32)
        sym = jnp.concatenate([sym_ref[...]] * (pairs // LANES), axis=1)
        kept = jnp.where(sym == occ, turned, 0.0).astype(BF16)
        out[...] = rows_dot(squeeze, kept).astype(BF16)


def multiply(rows_ref, kept_ref, k_ref, m_sym, keep_ref, send_ref):
    even = (lax.axis_index("col") & 1) == 0
    depth, chunk = k_ref.shape[1], 1024
    total = jnp.zeros((m_sym.shape[0], 256), F32)
    for at in range(0, depth, chunk):
        parts = []
        for start in range(at, at + chunk, LANES):
            lanes = slice(start, start + LANES)
            same = m_sym == jnp.broadcast_to(k_ref[0:1, lanes], m_sym.shape)
            parts.append(jnp.where(same, rows_ref[:, lanes], jnp.zeros((), BF16)))
        screened = jnp.concatenate(parts, axis=1)
        total += jnp.dot(screened, kept_ref[at : at + chunk, :], preferred_element_type=F32)
    turned = jnp.transpose(total)
    for z in range(4):
        for half in range(2):
            at = half * 128 + z * 2 * BASE
            low, high = turned[at : at + BASE, :], turned[at + BASE : at + 2 * BASE, :]
            slots = slice(half * BASE, half * BASE + BASE)
            keep_ref[z, slots, :] = jnp.where(even, low, high)
            send_ref[z, slots, :] = jnp.where(even, high, low)


def first_kernel(amp_ref, early, int_ref, k_ref, from_ref, m_ref, keep_ref, send_ref, kept, later, sem):
    core = lax.axis_index("col") & 1
    half = early.shape[0]
    fetch = pltpu.make_async_copy(int_ref.at[pl.ds(half, half)], later, sem)
    fetch.start()

    i, j = iota((256, 256), 0), iota((256, 256), 1)
    order = one_hot(j == (((i >> 1) & 1) ^ core) * 128 + (i >> 4) * 8 + ((i >> 2) & 3) * 2 + (i & 1))
    gap = jnp.zeros((256 - PLACES, 256), BF16)

    def unpack(source, carry):
        block = rows_dot(order, jnp.concatenate([amp_ref[source], gap], axis=0))
        at = [pl.ds(pl.multiple_of(r * 256 + source * 16, 16), 16) for r in range(16)]
        main = block[:, : 8 * BASE].astype(BF16)
        for r, rows in enumerate(at):
            shared = block[r * 16 : r * 16 + 16, 8 * BASE :]
            index = from_ref[rows, :]
            spilt = [jnp.take_along_axis(shared[h : h + 8], index[h : h + 8], axis=1) for h in (0, 8)]
            kept[rows, : 8 * BASE] = main[r * 16 : r * 16 + 16, :]
            kept[rows, 8 * BASE :] = jnp.concatenate(spilt, axis=0).astype(BF16)
        return carry

    lax.fori_loop(0, 16, unpack, 0, unroll=8)
    multiply(early, kept, k_ref, m_ref[:half, :], keep_ref, send_ref)
    fetch.wait()


def second_kernel(int_ref, kept_ref, k_ref, m_ref, keep_ref, send_ref):
    half = int_ref.shape[0]
    multiply(int_ref, kept_ref, k_ref, m_ref[half:, :], keep_ref, send_ref)


def share_kernel(keep_ref, got_ref, own_ref, *out_refs):
    z = lax.axis_index("col") >> 1
    own_ref[...] = keep_ref[z] + got_ref[z]
    for step, out_ref in enumerate(out_refs):
        there = (z + step + 1) & 3
        total = keep_ref[there] + got_ref[there]
        largest = jnp.max(jnp.abs(total), axis=0, keepdims=True)
        power = jnp.minimum(jnp.floor(14.9 - jnp.log2(jnp.maximum(largest, 1e-37))), 120.0)
        scaled = total * jnp.exp2(power)
        scaled = jnp.where(iota(total.shape, 0) == CAP - 1, power, scaled)
        out_ref[...] = (scaled + jnp.where(scaled >= 0, 0.5, -0.5)).astype(I32).astype(jnp.int16)


def expand_kernel(*refs):
    m_ref, occ_ref, rank_ref, out_ref = refs[-4:]
    lanes = pl.ds(pl.multiple_of(lax.axis_index("col") * LANES, LANES), LANES)
    slot = iota((CAP, LANES), 0)
    pick = one_hot(slot == jnp.broadcast_to(rank_ref[0:1, lanes], (CAP, LANES)))
    half = refs[0].shape[1]
    for part in range(2):
        total = refs[part * 4][...]
        for ref in refs[part * 4 + 1 : part * 4 + 4]:
            got = ref[...].astype(I32).astype(F32)
            total += got * jnp.exp2(-got[CAP - 1 : CAP, :])
        rows = slice(part * half, part * half + half)
        wide = lax.dot_general(total.astype(BF16), pick, (((0,), (0,)), ((), ())), preferred_element_type=F32)
        same = m_ref[rows, :].astype(F32) == jnp.broadcast_to(occ_ref[0:1, lanes].astype(F32), wide.shape)
        out_ref[rows, :] = jnp.where(same, wide, 0.0).astype(BF16)


def plain_symbols_kernel(
    occ_ref, virt_ref, occ_orbs, k_orbs, m_orbs, own_orbs, occ_out, rank_out, k_out, m_out, own_out, most_out
):
    occ = pack_labels(occ_ref[0:1, :])
    virt = pack_labels(virt_ref[0:7, :])
    first = lax.broadcasted_iota(I32, (LANES, LANES), 0)
    second = lax.broadcasted_iota(I32, (LANES, LANES), 1)
    most = jnp.zeros((1, LANES), I32)
    for start in range(0, occ_orbs.shape[1], LANES):
        sym = pair_symbols(occ, occ_orbs, start)
        occ_out[:, start : start + LANES] = sym
        same = as_column(sym) == jnp.broadcast_to(sym[0:1, :].astype(F32), (LANES, LANES))
        earlier = jnp.where(same & (first < second), 1.0, 0.0)
        rank = jnp.sum(earlier, axis=0, keepdims=True).astype(I32)
        most = jnp.maximum(most, rank)
        rank_out[:, start : start + LANES] = jnp.broadcast_to(rank, (8, LANES))
    most_out[0, 0] = jnp.max(most)
    for start in range(0, k_orbs.shape[1], LANES):
        sym = pair_symbols(virt, k_orbs, start).astype(F32)
        k_out[:, start : start + LANES] = jnp.concatenate([sym, sym], axis=0).astype(BF16)
    for start in range(0, m_orbs.shape[1], LANES):
        m_out[start : start + LANES, :] = as_column(pair_symbols(virt, m_orbs, start)).astype(BF16)
    for start in range(0, own_orbs.shape[1], LANES):
        own_out[start : start + LANES, :] = as_column(pair_symbols(virt, own_orbs, start)).astype(I32)


def plain_compact_kernel(copies, pass_ref, rows_ref, own_ref, occ_ref, rank_ref, out_ref):
    n, pairs = rows_ref.shape
    cols = pairs // LANES
    i = lax.broadcasted_iota(I32, (n, n), 0)
    j = lax.broadcasted_iota(I32, (n, n), 1)
    wanted = ((i >> 1) & 7) * 32 + (i >> 4) * 2 + (i & 1)
    order = jnp.where(j == wanted, 1.0, 0.0).astype(BF16)
    rows = jnp.dot(order, rows_ref[...], preferred_element_type=F32)
    base = pass_ref[0] * CAP
    slot = lax.broadcasted_iota(I32, (CAP, LANES), 0) + base
    own = own_ref[...]
    for c in range(cols):
        lanes = slice(c * LANES, (c + 1) * LANES)
        keep = own == jnp.broadcast_to(occ_ref[0:1, lanes], (n, LANES))
        kept = jnp.where(keep, rows[:, lanes], 0.0).astype(BF16)
        pick = jnp.where(slot == jnp.broadcast_to(rank_ref[0:1, lanes], (CAP, LANES)), 1.0, 0.0).astype(BF16)
        part = lax.dot_general(kept, pick, (((1,), (1,)), ((), ())), preferred_element_type=F32).astype(BF16)
        for r in range(copies):
            out_ref[r, :, c * CAP : (c + 1) * CAP] = part


def plain_product_kernel(core_ref, amp_ref, int_ref, k_ref, m_ref, keep_ref, send_ref, kept):
    depth, width = amp_ref.shape
    block = depth // 16

    @pl.when(pl.program_id(0) == 0)
    def _():
        for r in range(16):
            for source in range(16):
                kept[r * block + source * 16 : r * block + source * 16 + 16, :] = amp_ref[
                    source * block + r * 16 : source * block + r * 16 + 16, :
                ]

    m_sym = m_ref[...]
    chunk = 1024
    total = jnp.zeros((m_ref.shape[0], width), F32)
    for at in range(0, depth, chunk):
        parts = []
        for lane in range(at, at + chunk, LANES):
            lanes = slice(lane, lane + LANES)
            same = m_sym == jnp.broadcast_to(k_ref[0:1, lanes], m_sym.shape)
            parts.append(jnp.where(same, int_ref[:, lanes], jnp.zeros((), BF16)))
        screened = jnp.concatenate(parts, axis=1)
        total += jnp.dot(screened, kept[at : at + chunk, :], preferred_element_type=F32)
    turned = jnp.transpose(total)
    even = core_ref[0] == 0
    for z in range(4):
        low = turned[z * 2 * CAP : z * 2 * CAP + CAP, :]
        high = turned[z * 2 * CAP + CAP : z * 2 * CAP + 2 * CAP, :]
        keep_ref[z] = jnp.where(even, low, high)
        send_ref[z] = jnp.where(even, high, low)


def plain_share_kernel(z_ref, keep_ref, got_ref, *out_refs):
    for step, out_ref in enumerate(out_refs):
        z = (z_ref[0] + step) % 4
        out_ref[...] = keep_ref[z] + got_ref[z]


def plain_expand_kernel(at_ref, a_ref, b_ref, c_ref, d_ref, m_ref, occ_ref, rank_ref, out_ref):
    lanes = pl.ds(pl.multiple_of(at_ref[0] * LANES, LANES), LANES)
    total = (a_ref[...] + b_ref[...] + c_ref[...] + d_ref[...]).astype(BF16)
    slot = lax.broadcasted_iota(I32, (CAP, LANES), 0) + at_ref[1] * CAP
    pick = jnp.where(slot == jnp.broadcast_to(rank_ref[0:1, lanes], (CAP, LANES)), 1.0, 0.0).astype(BF16)
    wide = lax.dot_general(total, pick, (((0,), (0,)), ((), ())), preferred_element_type=F32)
    same = m_ref[...].astype(F32) == jnp.broadcast_to(occ_ref[0:1, lanes].astype(F32), wide.shape)
    out_ref[...] = jnp.where(same, wide, 0.0).astype(BF16)


def params(mib=16):
    return pltpu.CompilerParams(vmem_limit_bytes=mib * 1024 * 1024)


def whole():
    return pl.BlockSpec(memory_space=pltpu.VMEM)


def scalars():
    return pl.BlockSpec(memory_space=pltpu.SMEM)


def plain(amp_store, store_map, integrals, occ_irrep, virt_irrep, occ_orbs, k_orbs, m_orbs):
    rows = lax.axis_size("row")
    cols = lax.axis_size("col")
    stored, pairs = amp_store.shape
    kblock = k_orbs.shape[1]
    m_dev = m_orbs.shape[1]
    my_row = lax.axis_index("row")
    my_col = lax.axis_index("col")
    shape = jax.ShapeDtypeStruct

    place = (store_map // kblock) * (rows * 2) + ((store_map % kblock) // stored) * 2 + store_map % 2
    order = (jnp.arange(stored, dtype=I32)[:, None] == place[None, :]).astype(BF16)
    ordered = jnp.dot(order, amp_store, preferred_element_type=F32).astype(BF16)
    column_rows = lax.all_to_all(ordered, "col", split_axis=0, concat_axis=0, tiled=True)

    own_orbs = lax.dynamic_slice_in_dim(k_orbs.reshape(2, rows, stored), my_row * 16, 16, axis=2).reshape(2, stored)
    occ_lab = jnp.pad(occ_irrep, (0, LANES - occ_irrep.shape[0])).reshape(1, LANES)
    virt_lab = jnp.pad(virt_irrep, (0, 8 * LANES - virt_irrep.shape[0])).reshape(8, LANES)
    occ_sym, rank, k_sym, m_sym, own_sym, most = pl.pallas_call(
        plain_symbols_kernel,
        out_shape=(
            shape((8, pairs), I32),
            shape((8, pairs), I32),
            shape((16, kblock), BF16),
            shape((m_dev, LANES), BF16),
            shape((stored, LANES), I32),
            shape((1, 1), I32),
        ),
        in_specs=[whole()] * 6,
        out_specs=(whole(),) * 5 + (scalars(),),
        compiler_params=params(),
        name="plain_symbols",
    )(occ_lab, virt_lab, occ_orbs, k_orbs, m_orbs, own_orbs)

    def one_pass(step):
        width = cols * CAP
        compact = pl.pallas_call(
            functools.partial(plain_compact_kernel, rows),
            out_shape=shape((rows, stored, width), BF16),
            in_specs=[scalars()] + [whole()] * 4,
            out_specs=whole(),
            compiler_params=params(),
            name="plain_compact",
        )(step.reshape(1), column_rows, own_sym, occ_sym, rank)
        gathered = lax.all_to_all(
            compact.reshape(rows * stored, width), "row", split_axis=0, concat_axis=0, tiled=True
        )
        keep, send = pl.pallas_call(
            plain_product_kernel,
            grid=(m_dev // TM,),
            out_shape=(shape((4, CAP, m_dev), F32),) * 2,
            in_specs=[
                scalars(),
                pl.BlockSpec((kblock, width), lambda i: (0, 0)),
                pl.BlockSpec((TM, kblock), lambda i: (i, 0)),
                pl.BlockSpec((16, kblock), lambda i: (0, 0)),
                pl.BlockSpec((TM, LANES), lambda i: (i, 0)),
            ],
            out_specs=(pl.BlockSpec((4, CAP, TM), lambda i: (0, 0, i)),) * 2,
            scratch_shapes=[pltpu.VMEM((kblock, width), BF16)],
            compiler_params=params(),
            name="plain_product",
        )((my_col % 2).reshape(1), gathered, integrals, k_sym, m_sym)
        got = lax.ppermute(send, "col", [(i, i ^ 1) for i in range(cols)])
        shares = pl.pallas_call(
            plain_share_kernel,
            out_shape=(shape((CAP, m_dev), F32),) * 4,
            in_specs=[scalars(), whole(), whole()],
            out_specs=(whole(),) * 4,
            compiler_params=params(),
            name="plain_share",
        )((my_col // 2).reshape(1), keep, got)
        sums = [shares[0]]
        for distance in range(1, 4):
            hops = [(i, (i + 2 * distance) % cols) for i in range(cols)]
            sums.append(lax.ppermute(shares[distance], "col", hops))
        return pl.pallas_call(
            plain_expand_kernel,
            out_shape=shape((m_dev, LANES), BF16),
            in_specs=[scalars()] + [whole()] * 7,
            out_specs=whole(),
            compiler_params=params(),
            name="plain_expand",
        )(jnp.stack([my_col, step]), *sums, m_sym, occ_sym, rank)

    passes = most[0, 0] // CAP + 1
    return lax.while_loop(
        lambda state: state[0] < passes,
        lambda state: (state[0] + 1, state[1] + one_pass(state[0])),
        (jnp.zeros((), I32), jnp.zeros((m_dev, LANES), BF16)),
    )[1]


def body(amp_store, store_map, integrals, occ_irrep, virt_irrep, occ_orbs, k_orbs, m_orbs):
    rows = lax.axis_size("row")
    cols = lax.axis_size("col")
    stored, pairs = amp_store.shape
    kblock = k_orbs.shape[1]
    m_dev = m_orbs.shape[1]
    shape = jax.ShapeDtypeStruct
    swap = [(i, i ^ 1) for i in range(cols)]
    hops = [[(i, (i + 2 * d) % cols) for i in range(cols)] for d in range(4)]

    def call(kernel, name, out_shape, operands, mib=16, **kw):
        return pl.pallas_call(
            kernel,
            out_shape=out_shape,
            in_specs=kw.pop("in_specs", [whole()] * len(operands)),
            out_specs=kw.pop("out_specs", jax.tree.map(lambda _: whole(), out_shape)),
            compiler_params=params(mib),
            name=name,
            **kw,
        )(*operands)

    ordered = call(order_kernel, "order", (shape((64, pairs), BF16),) * 4, (store_map.reshape(1, stored), amp_store))
    arrived = [ordered[0]] + [lax.ppermute(ordered[d], "col", hops[d]) for d in range(1, 4)]

    other_orbs = lax.ppermute(k_orbs, "col", swap)
    labels = jnp.concatenate(
        [jnp.pad(virt_irrep, (0, 7 * LANES - virt_irrep.shape[0])), jnp.pad(occ_irrep, (0, LANES - occ_irrep.shape[0]))]
    ).reshape(8, LANES)
    half = m_dev // 2
    occ_sym, rank, place, origin, k_sym, own_sym, other_sym, early, bad = call(
        symbols_kernel,
        "symbols",
        (
            shape((8, pairs), I32),
            shape((8, pairs), I32),
            shape((8, pairs), I32),
            shape((kblock, LANES), I32),
            shape((16, kblock), BF16),
            shape((LANES, LANES), F32),
            shape((LANES, LANES), F32),
            shape((half, kblock), BF16),
            shape((1, 1), I32),
        ),
        (labels, occ_orbs, k_orbs, other_orbs, integrals),
        in_specs=[whole()] * 4 + [pl.BlockSpec(memory_space=pl.ANY)],
        out_specs=(whole(),) * 8 + (scalars(),),
        scratch_shapes=[
            pltpu.VMEM((kblock, LANES), BF16),
            pltpu.VMEM((kblock // 2, LANES), BF16),
            pltpu.SemaphoreType.DMA,
        ],
    )

    mine, theirs = call(
        compact_kernel,
        "compact",
        (shape((PLACES, LANES), BF16),) * 2,
        (*arrived, own_sym, other_sym, occ_sym, place),
    )
    got = lax.ppermute(theirs, "col", swap)
    later_labels, mine = lax.optimization_barrier((labels, mine))
    m_sym = call(outputs_kernel, "outputs", shape((m_dev, LANES), BF16), (later_labels, m_orbs))
    mine, m_sym = lax.optimization_barrier((mine, m_sym))
    spreading = jnp.broadcast_to(jnp.concatenate([mine, got], axis=1)[None], (rows, PLACES, stored))
    gathered = lax.all_to_all(spreading, "row", split_axis=0, concat_axis=0, tiled=True)

    pieces = (shape((4, CAP, half), F32),) * 2
    *first, kept, later = call(
        first_kernel,
        "first",
        pieces + (shape((kblock, 256), BF16), shape((half, kblock), BF16)),
        (gathered, early, integrals, k_sym, origin, m_sym),
        20,
        in_specs=[whole()] * 2 + [pl.BlockSpec(memory_space=pl.ANY)] + [whole()] * 3,
        scratch_shapes=[pltpu.SemaphoreType.DMA],
    )
    second = call(
        second_kernel,
        "second",
        pieces,
        (later, kept, k_sym, m_sym),
        12,
        cost_estimate=pl.CostEstimate(flops=half * kblock * 512, bytes_accessed=half * kblock * 2, transcendentals=0),
    )
    sums = []
    for keep, send in (first, second):
        partner = lax.ppermute(send, "col", swap)
        shares = call(
            share_kernel,
            "share",
            (shape((CAP, half), F32),) + (shape((CAP, half), jnp.int16),) * 3,
            (keep, partner),
        )
        sums += [shares[0]] + [lax.ppermute(shares[d], "col", hops[d]) for d in range(1, 4)]
    result = call(expand_kernel, "expand", shape((m_dev, LANES), BF16), (*sums, m_sym, occ_sym, rank))

    return lax.cond(
        bad[0, 0] > 0,
        lambda: plain(amp_store, store_map, integrals, occ_irrep, virt_irrep, occ_orbs, k_orbs, m_orbs),
        lambda: result,
    )


def solution(mesh):
    in_specs = (
        P(("row", "col"), None),
        P(("row", "col")),
        P("row", "col"),
        P(),
        P(),
        P(),
        P(None, "col"),
        P(None, "row"),
    )
    out_specs = P("row", "col")
    return jax.shard_map(body, mesh=mesh, in_specs=in_specs, out_specs=out_specs, check_vma=False)
```
